128 devices in a mesh: grp: 16 (over z, y), rep: 8 (over x, core).
Axes of the slice: x: 4, y: 4, z: 4, core: 2. Of those that a mesh axis runs over, the one named last changes fastest.
Arguments:
- user_feats: bfloat16 [8, 4096, 256], P('rep', 'grp'), may hold values from -6 to 6
- tower_in: bfloat16 [256, 512], replicated, may hold values from -0.375 to 0.375
- tower_out: bfloat16 [512, 512], replicated, may hold values from -0.4375 to 0.4375
- table_a: bfloat16 [1048576, 256], P(('grp', 'rep')), may hold values from -6 to 6
- table_b: bfloat16 [1048576, 256], P(('grp', 'rep')), may hold values from -6 to 6
- ask_rows: int32 [16, 8, 16, 8, 16], P('grp', 'rep'), may hold values from 0 to 8191
- slot_src: int32 [16, 8, 2048], P('grp', 'rep'), may hold values from 0 to 2047
- slot_req: int32 [16, 8, 2048], P('grp', 'rep'), may hold values from 0 to 4095
- live_counts: int32 [8, 16], P('rep', 'grp'), may hold values from 1 to 2048, 16384 in all within a row
- cross_w: bfloat16 [3, 1024, 1024], replicated, may hold values from -0.09375 to 0.09375
- cross_b: float32 [3, 1024], replicated, may hold values from -3 to 3
- head_w: bfloat16 [1024], replicated, may hold values from -0.1875 to 0.1875
Outputs:
- logits: float32 [16, 8, 2048], P('grp', 'rep')
The draws below stay inside these ranges and needn't reach their ends.
Inputs may be any that keep to these rules, and one draw needn't show every extreme that they name: `ask_rows`: owner-local row ids. `live_counts`: for each index of rep the counts sum to 16384, and one device of it has all 2048 slots live.
All inputs are finite; a program needn't handle non-finite values.
Results may differ from the reference program's by a relative error of at most 0.013.
Values may be sent and summed in bfloat16 or wider, within the bound.
A program may use at most 128 MiB of HBM per device.

```python
import math
import jax
import jax.numpy as jnp
import numpy as np
from jax import lax

E = 256
U = 512
UF = 256
X = 1024
LAYERS = 3
R_DEV = 256
SLOTS = 2048
CAP = 16
ROWS_DEV = 8192
VOCAB = 1048576
N_GRP = 16
N_REP = 8


def plant(result, rng, smallest, high):
    longest = result.shape.index(max(result.shape))
    spots = []
    for shift in (0, 1):
        where = [jax.random.randint(jax.random.fold_in(rng, axis), (), 0, length) for axis, length in enumerate(result.shape)]
        where[longest] = (where[longest] + shift) % result.shape[longest]
        spots.append(tuple(where))
    return result.at[spots[0]].set(smallest).at[spots[1]].set(high)


def block_levels(own_key, extent, pieces, smallest, top_value):
    factor_of = 1.0
    for axis_at, parts in pieces:
        steps = jax.random.uniform(jax.random.fold_in(jax.random.fold_in(own_key, 6), axis_at), (parts,), jnp.float32, smallest / len(pieces), top_value / len(pieces))
        factor_of = factor_of * jnp.repeat(jnp.exp(steps), extent[axis_at] // parts).reshape((-1,) + (1,) * (len(extent) - 1 - axis_at))
    return factor_of


def profile(count, total, bound, skew):
    loads = [(1 << 20) // math.isqrt(standing ** skew) + 1 for standing in range(2, count + 1)]
    surplus, holding = total - bound - (count - 1), [1] * (count - 1)
    while surplus > 0:
        movable = [i for i in range(count - 1) if holding[i] < bound]
        pool, left = sum([loads[i] for i in movable]), surplus
        for i in movable:
            extra = min(bound - holding[i], max(1, left * loads[i] // pool), surplus)
            holding[i] = holding[i] + extra
            surplus = surplus - extra
    return np.array([bound] + holding)


def uneven(own_key, count, total, bound, slope):
    if count == 2:
        one = jax.random.randint(own_key, (), max(1, total - bound), min(bound, total - 1) + 1)
        return jnp.stack([one, total - one])
    lengths = jnp.asarray(profile(count, total, bound, slope), jnp.int32)
    pairs = (count - 1) // 2
    source_of, receiver = lengths[1:1 + 2 * pairs:2], lengths[2:2 + 2 * pairs:2]
    margin = jnp.minimum(source_of - 1, bound - receiver)
    moved = jax.random.randint(jax.random.fold_in(own_key, 1), (pairs,), 0, 1 << 20) % (margin + 1)
    lengths = lengths.at[1:1 + 2 * pairs:2].set(source_of - moved).at[2:2 + 2 * pairs:2].set(receiver + moved)
    return lengths[jax.random.permutation(jax.random.fold_in(own_key, 2), count)]


def normal_values(stream_key, dims, spread, reach, split=(), kind=jnp.bfloat16):
    values = spread * jax.random.normal(stream_key, dims, jnp.float32)
    if split:
        values = values * block_levels(stream_key, dims, split, -0.22, 0.18)
    return jnp.clip(values, -reach, reach).astype(kind)


def setup_inputs(seed: int = 0) -> dict:
    arg_keys = jax.random.split(jax.random.key(seed), 13)
    user_feats = normal_values(arg_keys[0], (N_REP, N_GRP * R_DEV, UF), 1.0, 6.0, ((0, 8), (1, 16)))
    tower_in = normal_values(arg_keys[1], (UF, U), UF ** -0.5, 0.375)
    tower_out = normal_values(arg_keys[2], (U, U), (U // 3) ** -0.5, 0.4375)
    table_a = normal_values(arg_keys[3], (VOCAB, E), 1.0, 6.0, ((0, 128),))
    table_b = normal_values(arg_keys[4], (VOCAB, E), 1.0, 6.0, ((0, 128),))
    ask_rows = plant(jax.random.randint(arg_keys[5], (N_GRP, N_REP, N_GRP, N_REP, CAP), 0, ROWS_DEV), jax.random.fold_in(arg_keys[5], 1), 0, ROWS_DEV - 1).astype(jnp.int32)
    slot_src = plant(jax.random.randint(arg_keys[6], (N_GRP, N_REP, SLOTS), 0, N_GRP * N_REP * CAP), jax.random.fold_in(arg_keys[6], 1), 0, (N_GRP * N_REP * CAP) - 1).astype(jnp.int32)
    slot_req = plant(jax.random.randint(arg_keys[7], (N_GRP, N_REP, SLOTS), 0, N_GRP * R_DEV), jax.random.fold_in(arg_keys[7], 1), 0, (N_GRP * R_DEV) - 1).astype(jnp.int32)
    live_counts = jax.vmap(lambda own: uneven(own, N_GRP, N_GRP * SLOTS // 2, SLOTS, 2))(jax.random.split(arg_keys[8], N_REP)).reshape((N_REP, N_GRP)).astype(jnp.int32)
    cross_w = normal_values(arg_keys[9], (LAYERS, X, X), (4 * X) ** -0.5, 0.09375)
    cross_b = normal_values(arg_keys[10], (LAYERS, X), 0.5, 3.0, (), jnp.float32)
    head_w = normal_values(arg_keys[11], (X,), X ** -0.5, 0.1875)
    return {"user_feats": user_feats, "tower_in": tower_in, "tower_out": tower_out, "table_a": table_a, "table_b": table_b, "ask_rows": ask_rows, "slot_src": slot_src, "slot_req": slot_req, "live_counts": live_counts, "cross_w": cross_w, "cross_b": cross_b, "head_w": head_w}


def tower(feats, tower_in, tower_out):
    hidden = jax.nn.relu(jnp.dot(feats, tower_in, preferred_element_type=jnp.float32)).astype(jnp.bfloat16)
    return jnp.dot(hidden, tower_out, preferred_element_type=jnp.float32).astype(jnp.bfloat16)


def cross_stack(crossed_base, cross_w, cross_b, head_w):
    crossed = crossed_base
    base_wide = crossed_base.astype(jnp.float32)
    for layer_index in range(cross_w.shape[0]):
        mixed = jnp.dot(crossed, cross_w[layer_index], preferred_element_type=jnp.float32) + cross_b[layer_index]
        crossed = (base_wide * mixed + crossed.astype(jnp.float32)).astype(jnp.bfloat16)
    return jnp.dot(crossed, head_w, preferred_element_type=jnp.float32)


def reference(user_feats, tower_in, tower_out, table_a, table_b, ask_rows, slot_src, slot_req, live_counts, cross_w, cross_b, head_w):
    user_vecs = tower(user_feats.reshape(-1, UF), tower_in, tower_out).reshape(N_REP, N_GRP * R_DEV, U)
    span = N_GRP * N_REP * CAP

    def per_group(packed):
        sources, requests, asked, counts = packed
        local_rows = jnp.take_along_axis(asked.reshape(N_REP, span), sources, axis=1)
        global_rows = (sources // CAP) * ROWS_DEV + local_rows
        items = jnp.concatenate([jnp.take(table_a, global_rows, axis=0), jnp.take(table_b, global_rows, axis=0)], axis=-1)
        chosen = jax.vmap(lambda vectors, picks: jnp.take(vectors, picks, axis=0))(user_vecs, requests)
        crossed_base = jnp.concatenate([chosen, items], axis=-1)
        scores = cross_stack(crossed_base.reshape(-1, X), cross_w, cross_b, head_w).reshape(N_REP, SLOTS)
        live_mask = jnp.arange(SLOTS, dtype=jnp.int32)[None, :] < counts[:, None]
        return jnp.where(live_mask, scores, jnp.zeros_like(scores))

    return lax.map(per_group, (slot_src, slot_req, ask_rows, live_counts.T))
```

```python
import math

import jax
import jax.numpy as jnp
from jax import lax
from jax.experimental import pallas as pl
from jax.experimental.pallas import tpu as pltpu
from jax.sharding import PartitionSpec as P

MESH = pl.DeviceIdType.MESH
DMA = pltpu.SemaphoreType.DMA
BF16 = jnp.bfloat16
F32 = jnp.float32

CAP = 16
STEPS = 128
CHUNK_STEPS = 16
CHUNKS = STEPS // CHUNK_STEPS
TABLE_CHUNKS = 8


def remote(src, dst, send, recv, device):
    return pltpu.make_async_remote_copy(
        src_ref=src, dst_ref=dst, send_sem=send, recv_sem=recv, device_id=device, device_id_type=MESH
    )


def step_shift(i):
    dc, j = i % 2, i // 2
    a, b, e = j % 4, (j // 4) % 4, j // 16
    return (a + b + e) % 4, (a + b) % 4, a, dc


def exchange_kernel(
    feats_ref, table_a_ref, table_b_ref, asks_ref, rows_out, feats_out,
    tables, stage, ids_half, ids_mine, ids_smem, send_rows, recv_rows, rows_wide, feats_all,
    table_sem, local_sem, ids_send, ids_recv, ag_send, ag_recv, row_send, row_recv,
):
    g, r = lax.axis_index("grp"), lax.axis_index("rep")
    z, y, x, c = g // 4, g % 4, r // 2, r % 2
    g_line = [(g + i) % 16 for i in range(16)]
    r_line = [(r + i) % 8 for i in range(8)]
    y_line = [z * 4 + (y + i) % 4 for i in range(4)]
    z_line = [((z + i) % 4) * 4 + y for i in range(4)]

    span = tables.shape[0] // TABLE_CHUNKS
    table_copies = []
    for k in range(TABLE_CHUNKS):
        for t, ref in enumerate((table_a_ref, table_b_ref)):
            table_copies.append(
                pltpu.make_async_copy(
                    ref.at[pl.ds(k * span, span)],
                    stage.at[t, pl.ds(k * span, span)],
                    table_sem.at[t, k],
                )
            )
    for copy in table_copies:
        copy.start()

    barrier = pltpu.get_barrier_semaphore()
    for i in range(1, 8):
        pl.semaphore_signal(barrier, inc=1, device_id=(g, r_line[i]), device_id_type=MESH)
    for i in range(1, 16):
        pl.semaphore_signal(barrier, inc=1, device_id=(g_line[i], r), device_id_type=MESH)
    own_feats = feats_all.at[0, 0], feats_all.at[1, 0]
    feats_all[0, 0] = feats_ref[0:128]
    feats_all[1, 0] = feats_ref[128:256]
    pl.semaphore_wait(barrier, 22)

    first = [remote(asks_ref.at[:, r_line[i]], ids_half.at[:, r], ids_send.at[0], ids_recv.at[0], (g, r_line[i])) for i in range(1, 8)]
    for copy in first:
        copy.start()
    own = pltpu.make_async_copy(asks_ref.at[:, r], ids_half.at[:, r], local_sem.at[0])
    own.start()
    for i in (1, 3, 2):
        remote(own_feats[0], feats_all.at[0, i], ag_send, ag_recv.at[0, i], (y_line[i], r)).start()
        remote(own_feats[1], feats_all.at[1, 4 * i], ag_send, ag_recv.at[1, i], (z_line[i], r)).start()
    for i in (1, 3, 2):
        remote(own_feats[0], feats_all.at[0, 4 * i], ag_send, ag_recv.at[0, 0], (z_line[i], r)).start()
        remote(own_feats[1], feats_all.at[1, i], ag_send, ag_recv.at[1, 0], (y_line[i], r)).start()
    own.wait()
    pltpu.make_async_copy(ids_half.at[:, pl.ds(0, 7)], ids_half.at[:, pl.ds(0, 7)], ids_recv.at[0]).wait()
    for i in range(1, 16):
        remote(ids_half.at[g_line[i]], ids_mine.at[g], ids_send.at[1], ids_recv.at[1], (g_line[i], r)).start()
    own = pltpu.make_async_copy(ids_half.at[g], ids_mine.at[g], local_sem.at[0])
    own.start()
    for j in (1, 3, 2):
        remote(own_feats[0], feats_all.at[0, j], ag_send, ag_recv.at[0, j], (y_line[j], r)).wait_recv()
        for i in (1, 3, 2):
            remote(feats_all.at[0, j], feats_all.at[0, 4 * i + j], ag_send, ag_recv.at[0, 0], (z_line[i], r)).start()
        remote(own_feats[1], feats_all.at[1, 4 * j], ag_send, ag_recv.at[1, j], (z_line[j], r)).wait_recv()
        for i in (1, 3, 2):
            remote(feats_all.at[1, 4 * j], feats_all.at[1, 4 * j + i], ag_send, ag_recv.at[1, 0], (y_line[i], r)).start()

    for k in range(TABLE_CHUNKS):
        for t in range(2):
            table_copies[2 * k + t].wait()

        @pl.loop(0, span // 64)
        def _(j):
            at = pl.multiple_of(k * span + j * 64, 64)
            tables[pl.ds(at, 64), 0:256] = stage[0, pl.ds(at, 64), :].astype(F32)
            tables[pl.ds(at, 64), 256:512] = stage[1, pl.ds(at, 64), :].astype(F32)

    own.wait()
    pltpu.make_async_copy(ids_half.at[pl.ds(0, 15)], ids_mine.at[pl.ds(0, 15)], ids_recv.at[1]).wait()
    to_smem = pltpu.make_async_copy(ids_mine, ids_smem, local_sem.at[1])
    to_smem.start()
    to_smem.wait()

    def gathered(buffer, to_g, to_r):
        for k in range(CAP):
            row = ids_smem[to_g, to_r, 0, k]
            rows_wide[buffer, pl.ds(k, 1), :] = tables[pl.ds(row, 1), :]
        return rows_wide[buffer].astype(BF16)

    recv_rows[0] = gathered(0, g, r)

    def send_step(i, buffer):
        dz, dy, dx, dc = step_shift(i)
        to_g = ((z + dz) % 4) * 4 + (y + dy) % 4
        to_r = ((x + dx) % 4) * 2 + (c + dc) % 2
        send_rows[i] = gathered(buffer, to_g, to_r)
        remote(send_rows.at[i], recv_rows.at[i], row_send, row_recv.at[i // CHUNK_STEPS], (to_g, to_r)).start()

    send_step(1, 1)

    @pl.loop(1, STEPS // 2)
    def _(j):
        send_step(2 * j, 0)
        send_step(2 * j + 1, 1)

    for h in range(2):
        pltpu.make_async_copy(feats_all.at[h, pl.ds(0, 12)], feats_all.at[h, pl.ds(4, 12)], ag_recv.at[h, 0]).wait()
    for k in range(CHUNKS):
        n = CHUNK_STEPS - (k == 0)
        part = recv_rows.at[pl.ds(k * CHUNK_STEPS, n)]
        pltpu.make_async_copy(part, part, row_recv.at[k]).wait()
    rows_out[...] = recv_rows[...]
    feats_out[...] = feats_all[...]
    pltpu.make_async_copy(ids_half.at[:, pl.ds(0, 7)], ids_half.at[:, pl.ds(0, 7)], ids_send.at[0]).wait()
    pltpu.make_async_copy(ids_half.at[pl.ds(0, 15)], ids_mine.at[pl.ds(0, 15)], ids_send.at[1]).wait()
    for h in range(2):
        pltpu.make_async_copy(feats_all.at[h, pl.ds(0, 15)], feats_all.at[h, pl.ds(1, 15)], ag_send).wait()
    part = send_rows.at[pl.ds(0, STEPS - 1)]
    pltpu.make_async_copy(part, part, row_send).wait()


def exchange(feats, table_a, table_b, asks):
    vmem = pl.BlockSpec(memory_space=pltpu.VMEM)
    anywhere = pl.BlockSpec(memory_space=pl.ANY)
    rows_dev, e = table_a.shape
    return pl.pallas_call(
        exchange_kernel,
        out_shape=[
            jax.ShapeDtypeStruct((STEPS, CAP, 2 * e), BF16),
            jax.ShapeDtypeStruct((2, 16, 128, 256), BF16),
        ],
        in_specs=[vmem, anywhere, anywhere, vmem],
        out_specs=[vmem, vmem],
        scratch_shapes=[
            pltpu.VMEM((rows_dev, 2 * e), F32),
            pltpu.VMEM((2, rows_dev, e), BF16),
            pltpu.VMEM((16, 8, 1, CAP), jnp.int32),
            pltpu.VMEM((16, 8, 1, CAP), jnp.int32),
            pltpu.SMEM((16, 8, 1, CAP), jnp.int32),
            pltpu.VMEM((STEPS, CAP, 2 * e), BF16),
            pltpu.VMEM((STEPS, CAP, 2 * e), BF16),
            pltpu.VMEM((2, CAP, 2 * e), F32),
            pltpu.VMEM((2, 16, 128, 256), BF16),
            DMA((2, TABLE_CHUNKS)),
            DMA((2,)),
            DMA((2,)),
            DMA((2,)),
            DMA,
            DMA((2, 4)),
            DMA,
            DMA((CHUNKS,)),
        ],
        compiler_params=pltpu.CompilerParams(
            collective_id=0, has_side_effects=True, vmem_limit_bytes=52 * 1024 * 1024
        ),
    )(feats, table_a, table_b, asks)


def tower(feats, tower_in, tower_out):
    hidden = jax.nn.relu(jnp.dot(feats, tower_in, preferred_element_type=F32)).astype(BF16)
    return jnp.dot(hidden, tower_out, preferred_element_type=F32).astype(BF16)


def cross_stack(crossed_base, cross_w, cross_b, head_w):
    crossed = crossed_base
    base_wide = crossed_base.astype(F32)
    for layer_index in range(cross_w.shape[0]):
        mixed = jnp.dot(crossed, cross_w[layer_index], preferred_element_type=F32) + cross_b[layer_index]
        crossed = (base_wide * mixed + crossed.astype(F32)).astype(BF16)
    return jnp.dot(crossed, head_w, preferred_element_type=F32)


def select_rows(table, picks):
    count = picks.shape[0]
    block = math.gcd(count, 512)
    columns = jnp.arange(table.shape[0], dtype=jnp.int32)

    def one_block(block_picks):
        onehot = (block_picks[:, None] == columns[None, :]).astype(table.dtype)
        return jnp.dot(onehot, table, preferred_element_type=F32).astype(table.dtype)

    picked = lax.map(one_block, picks.reshape(count // block, block))
    return picked.reshape(count, table.shape[1])


def item_places(sources):
    g, r = lax.axis_index("grp"), lax.axis_index("rep")
    z, y, x, c = g // 4, g % 4, r // 2, r % 2
    owner, k = sources // CAP, sources % CAP
    og, o_r = owner // 8, owner % 8
    dz, dy = (z - og // 4) % 4, (y - og % 4) % 4
    dx, dc = (x - o_r // 2) % 4, (c - o_r % 2) % 2
    a, b, e = dx, (dy - dx) % 4, (dz - dy) % 4
    return ((e * 16 + b * 4 + a) * 2 + dc) * CAP + k


def request_places(requests):
    g = lax.axis_index("grp")
    z, y = g // 4, g % 4
    og = requests // 256
    slot = ((z - og // 4) % 4) * 4 + (y - og % 4) % 4
    return (requests // 128) % 2 * 2048 + slot * 128 + requests % 128


def body(
    user_feats, tower_in, tower_out, table_a, table_b, ask_rows, slot_src, slot_req, live_counts, cross_w, cross_b, head_w,
):
    rows, feats = exchange(user_feats[0], table_a, table_b, ask_rows.reshape(16, 8, 1, CAP))
    rows = rows.reshape(STEPS * CAP, rows.shape[-1])
    feats = feats.reshape(4096, feats.shape[-1])
    item_rows = select_rows(rows, item_places(slot_src[0, 0]))
    feat_rows = select_rows(feats, request_places(slot_req[0, 0]))
    user_rows = tower(feat_rows, tower_in, tower_out)
    crossed_base = jnp.concatenate([user_rows, item_rows], axis=-1)
    scores = cross_stack(crossed_base, cross_w, cross_b, head_w)
    live_mask = jnp.arange(scores.shape[0], dtype=jnp.int32) < live_counts[0, 0]
    return jnp.where(live_mask, scores, jnp.zeros_like(scores))[None, None, :]


def solution(mesh):
    return jax.shard_map(
        body,
        mesh=mesh,
        in_specs=(
            P("rep", "grp", None), P(), P(),
            P(("grp", "rep"), None), P(("grp", "rep"), None),
            P("grp", "rep", None, None, None), P("grp", "rep", None), P("grp", "rep", None),
            P("rep", "grp"), P(), P(), P(),
        ),
        out_specs=P("grp", "rep", None),
        check_vma=False,
    )
```

```python
import jax
import jax.numpy as jnp
from jax import lax
from jax.experimental import pallas as pl
from jax.experimental.pallas import tpu as pltpu
from jax.sharding import PartitionSpec as P

MESH = pl.DeviceIdType.MESH
DMA = pltpu.SemaphoreType.DMA
BF16 = jnp.bfloat16
F32 = jnp.float32

CAP = 16
STEPS = 128
CHUNK_STEPS = 16
CHUNKS = STEPS // CHUNK_STEPS
TABLE_CHUNKS = 8
TILE = 512


def remote(src, dst, send, recv, device):
    return pltpu.make_async_remote_copy(
        src_ref=src, dst_ref=dst, send_sem=send, recv_sem=recv, device_id=device, device_id_type=MESH
    )


def step_shift(i):
    dc, j = i % 2, i // 2
    a, b, e = j % 4, (j // 4) % 4, j // 16
    return (a + b + e) % 4, (a + b) % 4, a, dc


def dot(a, b):
    return jnp.dot(a, b, preferred_element_type=F32)


def item_places(sources, z, y, x, c):
    owner, k = sources // CAP, sources % CAP
    og, o_r = owner // 8, owner % 8
    dz, dy = (z - og // 4 + 4) % 4, (y - og % 4 + 4) % 4
    dx, dc = (x - o_r // 2 + 4) % 4, (c - o_r % 2 + 2) % 2
    a, b, e = dx, (dy - dx + 4) % 4, (dz - dy + 4) % 4
    return ((e * 16 + b * 4 + a) * 2 + dc) * CAP + k


def request_places(requests, z, y):
    og = requests // 256
    slot = ((z - og // 4 + 4) % 4) * 4 + (y - og % 4 + 4) % 4
    return (requests // 128) % 2 * 2048 + slot * 128 + requests % 128


def to_columns(places, columns):
    wide = places.astype(F32)
    for k in range(places.shape[0]):
        row = jnp.broadcast_to(wide[k : k + 1, :], (128, 128))
        columns[128 * k : 128 * (k + 1), :] = row.T


def onehot(column, first, width):
    lanes = lax.broadcasted_iota(jnp.int32, (1, 128), 1).astype(F32)
    parts = [
        jnp.where(column == lanes + (first + 128 * k), 1.0, 0.0).astype(BF16) for k in range(width // 128)
    ]
    return jnp.concatenate(parts, axis=1)


def ranking_kernel(
    feats_ref, tower_in_ref, tower_out_ref, table_a_ref, table_b_ref, asks_ref, src_ref, req_ref, live_ref,
    cross_w_ref, cross_b_ref, head_ref, logits_ref,
    tables, stage, ids_half, ids_mine, ids_smem, send_rows, recv_rows, rows_wide, feats_all,
    cross_w, tower_in, tower_out, flipped, src_col, req_col, user, items,
    table_sem, weight_sem, local_sem, ids_send, ids_recv, ag_send, ag_recv, row_send, row_recv,
):
    g, r = lax.axis_index("grp"), lax.axis_index("rep")
    z, y, x, c = g // 4, g % 4, r // 2, r % 2
    g_line = [(g + i) % 16 for i in range(16)]
    r_line = [(r + i) % 8 for i in range(8)]
    y_line = [z * 4 + (y + i) % 4 for i in range(4)]
    z_line = [((z + i) % 4) * 4 + y for i in range(4)]

    span = tables.shape[0] // TABLE_CHUNKS
    table_copies = []
    for k in range(TABLE_CHUNKS):
        for t, ref in enumerate((table_a_ref, table_b_ref)):
            table_copies.append(
                pltpu.make_async_copy(
                    ref.at[pl.ds(k * span, span)],
                    stage.at[t, pl.ds(k * span, span)],
                    table_sem.at[t, k],
                )
            )
    for copy in table_copies:
        copy.start()
    weight_copies = [
        pltpu.make_async_copy(ref, scratch, weight_sem.at[n])
        for n, (ref, scratch) in enumerate(
            ((tower_in_ref, tower_in), (tower_out_ref, tower_out), (cross_w_ref, cross_w))
        )
    ]
    for copy in weight_copies:
        copy.start()

    barrier = pltpu.get_barrier_semaphore()
    for i in range(1, 8):
        pl.semaphore_signal(barrier, inc=1, device_id=(g, r_line[i]), device_id_type=MESH)
    for i in range(1, 16):
        pl.semaphore_signal(barrier, inc=1, device_id=(g_line[i], r), device_id_type=MESH)
    own_feats = feats_all.at[0], feats_all.at[16]
    feats_all[0] = feats_ref[0:128]
    feats_all[16] = feats_ref[128:256]
    pl.semaphore_wait(barrier, 22)

    first = [remote(asks_ref.at[:, r_line[i]], ids_half.at[:, r], ids_send.at[0], ids_recv.at[0], (g, r_line[i])) for i in range(1, 8)]
    for copy in first:
        copy.start()
    own = pltpu.make_async_copy(asks_ref.at[:, r], ids_half.at[:, r], local_sem.at[0])
    own.start()
    for i in (1, 3, 2):
        remote(own_feats[0], feats_all.at[i], ag_send, ag_recv.at[0, i], (y_line[i], r)).start()
        remote(own_feats[1], feats_all.at[16 + 4 * i], ag_send, ag_recv.at[1, i], (z_line[i], r)).start()
    for i in (1, 3, 2):
        remote(own_feats[0], feats_all.at[4 * i], ag_send, ag_recv.at[0, 0], (z_line[i], r)).start()
        remote(own_feats[1], feats_all.at[16 + i], ag_send, ag_recv.at[1, 0], (y_line[i], r)).start()
    own.wait()
    pltpu.make_async_copy(ids_half.at[:, pl.ds(0, 7)], ids_half.at[:, pl.ds(0, 7)], ids_recv.at[0]).wait()
    for i in range(1, 16):
        remote(ids_half.at[g_line[i]], ids_mine.at[g], ids_send.at[1], ids_recv.at[1], (g_line[i], r)).start()
    own = pltpu.make_async_copy(ids_half.at[g], ids_mine.at[g], local_sem.at[0])
    own.start()
    for j in (1, 3, 2):
        remote(own_feats[0], feats_all.at[j], ag_send, ag_recv.at[0, j], (y_line[j], r)).wait_recv()
        for i in (1, 3, 2):
            remote(feats_all.at[j], feats_all.at[4 * i + j], ag_send, ag_recv.at[0, 0], (z_line[i], r)).start()
        remote(own_feats[1], feats_all.at[16 + 4 * j], ag_send, ag_recv.at[1, j], (z_line[j], r)).wait_recv()
        for i in (1, 3, 2):
            remote(feats_all.at[16 + 4 * j], feats_all.at[16 + 4 * j + i], ag_send, ag_recv.at[1, 0], (y_line[i], r)).start()

    for k in range(TABLE_CHUNKS):
        for t in range(2):
            table_copies[2 * k + t].wait()

        @pl.loop(0, span // 64)
        def _(j):
            at = pl.multiple_of(k * span + j * 64, 64)
            tables[pl.ds(at, 64), 0:256] = stage[0, pl.ds(at, 64), :].astype(F32)
            tables[pl.ds(at, 64), 256:512] = stage[1, pl.ds(at, 64), :].astype(F32)

    own.wait()
    pltpu.make_async_copy(ids_half.at[pl.ds(0, 15)], ids_mine.at[pl.ds(0, 15)], ids_recv.at[1]).wait()
    to_smem = pltpu.make_async_copy(ids_mine, ids_smem, local_sem.at[1])
    to_smem.start()
    to_smem.wait()

    def gathered(buffer, to_g, to_r):
        for k in range(CAP):
            row = ids_smem[to_g, to_r, 0, k]
            rows_wide[buffer, pl.ds(k, 1), :] = tables[pl.ds(row, 1), :]
        return rows_wide[buffer].astype(BF16)

    recv_rows[0] = gathered(0, g, r)

    def send_step(i, buffer):
        dz, dy, dx, dc = step_shift(i)
        to_g = ((z + dz) % 4) * 4 + (y + dy) % 4
        to_r = ((x + dx) % 4) * 2 + (c + dc) % 2
        send_rows[i] = gathered(buffer, to_g, to_r)
        remote(send_rows.at[i], recv_rows.at[i], row_send, row_recv.at[i // CHUNK_STEPS], (to_g, to_r)).start()

    send_step(1, 1)

    @pl.loop(1, STEPS // 2)
    def _(j):
        send_step(2 * j, 0)
        send_step(2 * j + 1, 1)

    to_columns(item_places(src_ref[...], z, y, x, c), src_col)
    to_columns(request_places(req_ref[...], z, y), req_col)
    for copy in weight_copies:
        copy.wait()
    head = head_ref[...].astype(F32)
    flipped[...] = (cross_w[2].astype(F32) * head).T.astype(BF16)
    for h in range(2):
        pltpu.make_async_copy(
            feats_all.at[pl.ds(0, 12)], feats_all.at[pl.ds(0, 12)], ag_recv.at[h, 0]
        ).wait()
    slots, half = user.shape
    bias = cross_b_ref[...]

    @pl.loop(0, slots // TILE)
    def _(t):
        at = pl.ds(pl.multiple_of(t * TILE, TILE), TILE)
        column = req_col[at, :]
        picked = jnp.zeros((TILE, 256), F32)
        for k in range(4):
            picked += dot(onehot(column, 1024 * k, 1024), feats_all[8 * k : 8 * (k + 1)].reshape(1024, 256))
        hidden = jnp.maximum(dot(picked.astype(BF16), tower_in[...]), 0.0).astype(BF16)
        vec = dot(hidden, tower_out[...]).astype(BF16)
        user[at, :] = vec
        for n in range(2):
            cols = slice(half * n, half * (n + 1))
            mixed = dot(vec, cross_w[0, 0:half, cols]) + (bias[0:1, cols] + 1.0)
            turned = dot(vec, flipped[0:half, cols]) + head[:, cols]
            tables[pl.ds(pl.multiple_of(n * slots + t * TILE, TILE), TILE), :] = mixed
            tables[pl.ds(pl.multiple_of((n + 2) * slots + t * TILE, TILE), TILE), :] = turned

    for k in range(CHUNKS):
        n = CHUNK_STEPS - (k == 0)
        part = recv_rows.at[pl.ds(k * CHUNK_STEPS, n)]
        pltpu.make_async_copy(part, part, row_recv.at[k]).wait()
        width = CHUNK_STEPS * CAP

        @pl.loop(0, slots // TILE)
        def _(t):
            at = pl.ds(pl.multiple_of(t * TILE, TILE), TILE)
            rows = recv_rows[k * CHUNK_STEPS : (k + 1) * CHUNK_STEPS].reshape(width, half)
            picked = dot(onehot(src_col[at, :], k * width, width), rows)
            items[at, :] = picked if k == 0 else items[at, :] + picked

    live = live_ref[0, 0]
    by_bias = head * bias[2:3, :]

    @pl.loop(0, slots // TILE)
    def _(t):
        at = pl.ds(pl.multiple_of(t * TILE, TILE), TILE)
        item = items[at, :].astype(BF16)
        base = (user[at, :], item)
        crossed, turned = [], []
        for n in range(2):
            cols = slice(half * n, half * (n + 1))
            mixed = dot(item, cross_w[0, half:, cols]) + tables[pl.ds(pl.multiple_of(n * slots + t * TILE, TILE), TILE), :]
            crossed.append((base[n].astype(F32) * mixed).astype(BF16))
        crossed_1 = jnp.concatenate(crossed, axis=1)
        total = jnp.zeros((TILE, 128), F32)
        for n in range(2):
            cols = slice(half * n, half * (n + 1))
            wide = base[n].astype(F32)
            mixed = dot(crossed_1, cross_w[1, :, cols]) + bias[1:2, cols]
            crossed_2 = (wide * mixed + crossed[n].astype(F32)).astype(BF16).astype(F32)
            turned = dot(item, flipped[half:, cols]) + tables[pl.ds(pl.multiple_of((n + 2) * slots + t * TILE, TILE), TILE), :]
            score = crossed_2 * turned + wide * by_bias[:, cols]
            for m in range(half // 128):
                total += score[:, 128 * m : 128 * (m + 1)]
        for m in range(TILE // 128):
            scores = jnp.sum(total[128 * m : 128 * (m + 1), :].T, axis=0, keepdims=True)
            first = t * TILE + m * 128
            spots = lax.broadcasted_iota(jnp.int32, (1, 128), 1) + first
            logits_ref[pl.ds(t * (TILE // 128) + m, 1), :] = jnp.where(spots < live, scores, 0.0)

    pltpu.make_async_copy(ids_half.at[:, pl.ds(0, 7)], ids_half.at[:, pl.ds(0, 7)], ids_send.at[0]).wait()
    pltpu.make_async_copy(ids_half.at[pl.ds(0, 15)], ids_mine.at[pl.ds(0, 15)], ids_send.at[1]).wait()
    pltpu.make_async_copy(feats_all.at[pl.ds(0, 30)], feats_all.at[pl.ds(0, 30)], ag_send).wait()
    part = send_rows.at[pl.ds(0, STEPS - 1)]
    pltpu.make_async_copy(part, part, row_send).wait()


def body(
    user_feats, tower_in, tower_out, table_a, table_b, ask_rows, slot_src, slot_req, live_counts, cross_w, cross_b, head_w,
):
    vmem = pl.BlockSpec(memory_space=pltpu.VMEM)
    smem = pl.BlockSpec(memory_space=pltpu.SMEM)
    anywhere = pl.BlockSpec(memory_space=pl.ANY)
    rows_dev, e = table_a.shape
    slots = slot_src.shape[-1]
    x = cross_w.shape[-1]
    logits = pl.pallas_call(
        ranking_kernel,
        out_shape=jax.ShapeDtypeStruct((slots // 128, 128), F32),
        in_specs=[vmem, anywhere, anywhere, anywhere, anywhere, vmem, vmem, vmem, smem, anywhere, vmem, vmem],
        out_specs=vmem,
        scratch_shapes=[
            pltpu.VMEM((rows_dev, 2 * e), F32),
            pltpu.VMEM((2, rows_dev, e), BF16),
            pltpu.VMEM((16, 8, 1, CAP), jnp.int32),
            pltpu.VMEM((16, 8, 1, CAP), jnp.int32),
            pltpu.SMEM((16, 8, 1, CAP), jnp.int32),
            pltpu.VMEM((STEPS, CAP, 2 * e), BF16),
            pltpu.VMEM((STEPS, CAP, 2 * e), BF16),
            pltpu.VMEM((2, CAP, 2 * e), F32),
            pltpu.VMEM((32, 128, user_feats.shape[-1]), BF16),
            pltpu.VMEM(cross_w.shape, BF16),
            pltpu.VMEM(tower_in.shape, BF16),
            pltpu.VMEM(tower_out.shape, BF16),
            pltpu.VMEM((x, x), BF16),
            pltpu.VMEM((slots, 128), F32),
            pltpu.VMEM((slots, 128), F32),
            pltpu.VMEM((slots, x // 2), BF16),
            pltpu.VMEM((slots, x // 2), F32),
            DMA((2, TABLE_CHUNKS)),
            DMA((3,)),
            DMA((2,)),
            DMA((2,)),
            DMA((2,)),
            DMA,
            DMA((2, 4)),
            DMA,
            DMA((CHUNKS,)),
        ],
        compiler_params=pltpu.CompilerParams(
            collective_id=0, has_side_effects=True, vmem_limit_bytes=60 * 1024 * 1024
        ),
    )(
        user_feats[0], tower_in, tower_out, table_a, table_b, ask_rows.reshape(16, 8, 1, CAP),
        slot_src.reshape(slots // 128, 128), slot_req.reshape(slots // 128, 128), live_counts,
        cross_w, cross_b, head_w.reshape(1, x),
    )
    return logits.reshape(1, 1, slots)


def solution(mesh):
    return jax.shard_map(
        body,
        mesh=mesh,
        in_specs=(
            P("rep", "grp", None), P(), P(),
            P(("grp", "rep"), None), P(("grp", "rep"), None),
            P("grp", "rep", None, None, None), P("grp", "rep", None), P("grp", "rep", None),
            P("rep", "grp"), P(), P(), P(),
        ),
        out_specs=P("grp", "rep", None),
        check_vma=False,
    )
```

```python
import jax
import jax.numpy as jnp
from jax import lax
from jax.experimental import pallas as pl
from jax.experimental.pallas import tpu as pltpu
from jax.sharding import PartitionSpec as P

MESH = pl.DeviceIdType.MESH
DMA = pltpu.SemaphoreType.DMA
BF16 = jnp.bfloat16
F32 = jnp.float32

CAP = 16
STEPS = 128
GROUP = 8
PARTS = (0, 32, 64, 112, 128)
CHUNKS = len(PARTS) - 1
TABLE_CHUNKS = 8
TILE = 1024


def remote(src, dst, send, recv, device):
    return pltpu.make_async_remote_copy(
        src_ref=src, dst_ref=dst, send_sem=send, recv_sem=recv, device_id=device, device_id_type=MESH
    )


def dot(a, b):
    return jnp.dot(a, b, preferred_element_type=F32)


def item_places(sources, z, y, x, c):
    owner, k = sources // CAP, sources % CAP
    og, o_r = owner // 8, owner % 8
    dz, dy = (z - og // 4 + 4) % 4, (y - og % 4 + 4) % 4
    dx, dc = (x - o_r // 2 + 4) % 4, (c - o_r % 2 + 2) % 2
    a, b, e = dx, (dy - dx + 4) % 4, (dz - dy + 4) % 4
    return ((e * 16 + b * 4 + a) * 2 + dc) * CAP + k


def request_places(requests, z, y):
    og = requests // 256
    slot = ((z - og // 4 + 4) % 4) * 4 + (y - og % 4 + 4) % 4
    return (requests // 128) % 2 * 2048 + slot * 128 + requests % 128


def to_columns(places, columns):
    wide = places.astype(F32)
    for k in range(places.shape[0]):
        row = jnp.broadcast_to(wide[k : k + 1, :], (128, 128))
        columns[128 * k : 128 * (k + 1), :] = row.T


def onehot(column, first, width):
    lanes = lax.broadcasted_iota(jnp.int32, (1, 128), 1).astype(F32)
    parts = [
        jnp.where(column == lanes + (first + 128 * k), 1.0, 0.0).astype(BF16) for k in range(width // 128)
    ]
    return jnp.concatenate(parts, axis=1)


def ranking_kernel(
    feats_ref, tower_in_ref, tower_out_ref, table_a_ref, table_b_ref, asks_ref, src_ref, req_ref,
    cross_w_ref, cross_b_ref, head_ref, logits_ref,
    tables, stage, ids_half, ids_mine, ids_smem, send_rows, recv_rows, rows_wide, feats_all,
    cross_w, tower_in, tower_out, flipped, src_col, req_col, user, items,
    table_sem, weight_sem, local_sem, ids_send, ids_recv, ag_send, ag_recv, row_send, row_recv,
):
    g, r = lax.axis_index("grp"), lax.axis_index("rep")
    z, y, x, c = g // 4, g % 4, r // 2, r % 2
    g_line = [(g + i) % 16 for i in range(16)]
    r_line = [(r + i) % 8 for i in range(8)]
    y_line = [z * 4 + (y + i) % 4 for i in range(4)]
    z_line = [((z + i) % 4) * 4 + y for i in range(4)]

    span = tables.shape[0] // TABLE_CHUNKS
    table_copies = []
    for k in range(TABLE_CHUNKS):
        for t, ref in enumerate((table_a_ref, table_b_ref)):
            table_copies.append(
                pltpu.make_async_copy(
                    ref.at[pl.ds(k * span, span)],
                    stage.at[t, pl.ds(k * span, span)],
                    table_sem.at[t, k],
                )
            )
    for copy in table_copies:
        copy.start()
    weight_copies = [
        pltpu.make_async_copy(ref, scratch, weight_sem.at[n])
        for n, (ref, scratch) in enumerate(
            ((tower_in_ref, tower_in), (tower_out_ref, tower_out), (cross_w_ref, cross_w))
        )
    ]
    for copy in weight_copies:
        copy.start()

    barrier = pltpu.get_barrier_semaphore()
    for i in range(1, 8):
        pl.semaphore_signal(barrier, inc=1, device_id=(g, r_line[i]), device_id_type=MESH)
    for i in range(1, 16):
        pl.semaphore_signal(barrier, inc=1, device_id=(g_line[i], r), device_id_type=MESH)
    own_feats = feats_all.at[0], feats_all.at[16]
    feats_all[0] = feats_ref[0:128]
    feats_all[16] = feats_ref[128:256]
    pl.semaphore_wait(barrier, 22)

    first = [remote(asks_ref.at[:, r_line[i]], ids_half.at[:, r], ids_send.at[0], ids_recv.at[0], (g, r_line[i])) for i in range(1, 8)]
    for copy in first:
        copy.start()
    own = pltpu.make_async_copy(asks_ref.at[:, r], ids_half.at[:, r], local_sem.at[0])
    own.start()
    for i in (1, 3, 2):
        remote(own_feats[0], feats_all.at[i], ag_send, ag_recv.at[0, i], (y_line[i], r)).start()
        remote(own_feats[1], feats_all.at[16 + 4 * i], ag_send, ag_recv.at[1, i], (z_line[i], r)).start()
    for i in (1, 3, 2):
        remote(own_feats[0], feats_all.at[4 * i], ag_send, ag_recv.at[0, 0], (z_line[i], r)).start()
        remote(own_feats[1], feats_all.at[16 + i], ag_send, ag_recv.at[1, 0], (y_line[i], r)).start()
    for k in range(TABLE_CHUNKS):
        for t in range(2):
            table_copies[2 * k + t].wait()

        @pl.loop(0, span // 64)
        def _(j):
            at = pl.multiple_of(k * span + j * 64, 64)
            tables[pl.ds(at, 64), 0:256] = stage[0, pl.ds(at, 64), :].astype(F32)
            tables[pl.ds(at, 64), 256:512] = stage[1, pl.ds(at, 64), :].astype(F32)

    own.wait()
    pltpu.make_async_copy(ids_half.at[:, pl.ds(0, 7)], ids_half.at[:, pl.ds(0, 7)], ids_recv.at[0]).wait()
    for i in range(1, 16):
        remote(ids_half.at[g_line[i]], ids_mine.at[g], ids_send.at[1], ids_recv.at[1], (g_line[i], r)).start()
    own = pltpu.make_async_copy(ids_half.at[g], ids_mine.at[g], local_sem.at[0])
    own.start()
    for j in (1, 3, 2):
        remote(own_feats[0], feats_all.at[j], ag_send, ag_recv.at[0, j], (y_line[j], r)).wait_recv()
        for i in (1, 3, 2):
            remote(feats_all.at[j], feats_all.at[4 * i + j], ag_send, ag_recv.at[0, 0], (z_line[i], r)).start()
        remote(own_feats[1], feats_all.at[16 + 4 * j], ag_send, ag_recv.at[1, j], (z_line[j], r)).wait_recv()
        for i in (1, 3, 2):
            remote(feats_all.at[16 + 4 * j], feats_all.at[16 + 4 * j + i], ag_send, ag_recv.at[1, 0], (y_line[i], r)).start()

    slots, half = user.shape
    bias = cross_b_ref[...]
    head = head_ref[...].astype(F32).reshape(1, 2 * half)
    to_columns(item_places(src_ref[...], z, y, x, c), src_col)
    to_columns(request_places(req_ref[...], z, y), req_col)
    for copy in weight_copies:
        copy.wait()
    flipped[...] = (cross_w[2].astype(F32) * head).T.astype(BF16)

    own.wait()
    pltpu.make_async_copy(ids_half.at[pl.ds(0, 15)], ids_mine.at[pl.ds(0, 15)], ids_recv.at[1]).wait()
    to_smem = pltpu.make_async_copy(ids_mine, ids_smem, local_sem.at[1])
    to_smem.start()
    to_smem.wait()

    r_hops = [((x + hop) % 4) * 2 + (c + dc) % 2 for hop in range(4) for dc in range(2)]

    def partner(j, m):
        hop_y = m // 2 + j % 4
        hop_z = hop_y + j // 4
        return ((z + hop_z) % 4) * 4 + (y + hop_y) % 4, r_hops[m]

    @pl.loop(0, STEPS // GROUP)
    def _(j):
        for m in range(GROUP):
            to_g, to_r = partner(j, m)
            for k in range(CAP):
                rows_wide[m % 2, pl.ds(k, 1), :] = tables[pl.ds(ids_smem[to_g, to_r, 0, k], 1), :]
            send_rows[j * GROUP + m] = rows_wide[m % 2].astype(BF16)

    recv_rows[0] = send_rows[0]

    for h in range(2):
        pltpu.make_async_copy(
            feats_all.at[pl.ds(0, 12)], feats_all.at[pl.ds(0, 12)], ag_recv.at[h, 0]
        ).wait()

    def send_step(j, m, part):
        i = j * GROUP + m
        remote(send_rows.at[i], recv_rows.at[i], row_send, row_recv.at[part], partner(j, m)).start()

    for m in range(1, GROUP):
        send_step(0, m, 0)
    for k in range(CHUNKS):

        @pl.loop(max(PARTS[k] // GROUP, 1), PARTS[k + 1] // GROUP)
        def _(j):
            for m in range(GROUP):
                send_step(j, m, k)

    def arrived(k):
        part = recv_rows.at[pl.ds(max(PARTS[k], 1), PARTS[k + 1] - max(PARTS[k], 1))]
        pltpu.make_async_copy(part, part, row_recv.at[k]).wait()

    def tile(t, first=0):
        return pl.ds(pl.multiple_of(first + t * TILE, TILE), TILE)

    def picked(t, k):
        first, width = PARTS[k] * CAP, (PARTS[k + 1] - PARTS[k]) * CAP
        rows = recv_rows[PARTS[k] : PARTS[k + 1]].reshape(width, half)
        return dot(onehot(src_col[tile(t), :], first, width), rows)

    def pick_part(k):
        arrived(k)

        @pl.loop(0, slots // TILE)
        def _(t):
            items[tile(t), :] = picked(t, k) if k == 0 else items[tile(t), :] + picked(t, k)

    @pl.loop(0, slots // TILE)
    def _(t):
        places = onehot(req_col[tile(t), :], 0, 4096)
        user[tile(t), 0:256] = dot(places, feats_all[...].reshape(4096, 256)).astype(BF16)

    @pl.loop(0, slots // TILE)
    def _(t):
        hidden = jnp.maximum(dot(user[tile(t), 0:256], tower_in[...]), 0.0).astype(BF16)
        user[tile(t), :] = dot(hidden, tower_out[...]).astype(BF16)

    @pl.loop(0, slots // TILE)
    def _(t):
        vec = user[tile(t), :]
        for n in range(2):
            cols = slice(half * n, half * (n + 1))
            tables[tile(t, n * slots), :] = dot(vec, cross_w[0, 0:half, cols]) + (bias[0:1, cols] + 1.0)
            tables[tile(t, (n + 2) * slots), :] = dot(vec, flipped[0:half, cols]) + head[:, cols]

    for k in range(CHUNKS - 1):
        pick_part(k)
    arrived(CHUNKS - 1)

    by_bias = head * bias[2:3, :]

    @pl.loop(0, slots // TILE)
    def _(t):
        item = (items[tile(t), :] + picked(t, CHUNKS - 1)).astype(BF16)
        base = (user[tile(t), :], item)
        crossed = []
        for n in range(2):
            cols = slice(half * n, half * (n + 1))
            mixed = dot(item, cross_w[0, half:, cols]) + tables[tile(t, n * slots), :]
            crossed.append((base[n].astype(F32) * mixed).astype(BF16))
        crossed_1 = jnp.concatenate(crossed, axis=1)
        total = jnp.zeros((TILE, 128), F32)
        for n in range(2):
            cols = slice(half * n, half * (n + 1))
            wide = base[n].astype(F32)
            mixed = dot(crossed_1, cross_w[1, :, cols]) + bias[1:2, cols]
            crossed_2 = (wide * mixed + crossed[n].astype(F32)).astype(BF16).astype(F32)
            turned = dot(item, flipped[half:, cols]) + tables[tile(t, (n + 2) * slots), :]
            score = crossed_2 * turned + wide * by_bias[:, cols]
            for m in range(half // 128):
                total += score[:, 128 * m : 128 * (m + 1)]
        for m in range(TILE // 128):
            logits_ref[pl.ds(t * (TILE // 128) + m, 1), :] = jnp.sum(
                total[128 * m : 128 * (m + 1), :].T, axis=0, keepdims=True
            )

    pltpu.make_async_copy(ids_half.at[:, pl.ds(0, 7)], ids_half.at[:, pl.ds(0, 7)], ids_send.at[0]).wait()
    pltpu.make_async_copy(ids_half.at[pl.ds(0, 15)], ids_mine.at[pl.ds(0, 15)], ids_send.at[1]).wait()
    pltpu.make_async_copy(feats_all.at[pl.ds(0, 30)], feats_all.at[pl.ds(0, 30)], ag_send).wait()
    part = send_rows.at[pl.ds(0, STEPS - 1)]
    pltpu.make_async_copy(part, part, row_send).wait()


def body(
    user_feats, tower_in, tower_out, table_a, table_b, ask_rows, slot_src, slot_req, live_counts, cross_w, cross_b, head_w,
):
    vmem = pl.BlockSpec(memory_space=pltpu.VMEM)
    anywhere = pl.BlockSpec(memory_space=pl.ANY)
    rows_dev, e = table_a.shape
    slots = slot_src.shape[-1]
    x = cross_w.shape[-1]
    logits = pl.pallas_call(
        ranking_kernel,
        out_shape=jax.ShapeDtypeStruct((slots // 128, 128), F32),
        in_specs=[vmem, anywhere, anywhere, anywhere, anywhere, vmem, vmem, vmem, anywhere, vmem, vmem],
        out_specs=vmem,
        scratch_shapes=[
            pltpu.VMEM((rows_dev, 2 * e), F32),
            pltpu.VMEM((2, rows_dev, e), BF16),
            pltpu.VMEM((16, 8, 1, CAP), jnp.int32),
            pltpu.VMEM((16, 8, 1, CAP), jnp.int32),
            pltpu.SMEM((16, 8, 1, CAP), jnp.int32),
            pltpu.VMEM((STEPS, CAP, 2 * e), BF16),
            pltpu.VMEM((STEPS, CAP, 2 * e), BF16),
            pltpu.VMEM((2, CAP, 2 * e), F32),
            pltpu.VMEM((32, 128, user_feats.shape[-1]), BF16),
            pltpu.VMEM(cross_w.shape, BF16),
            pltpu.VMEM(tower_in.shape, BF16),
            pltpu.VMEM(tower_out.shape, BF16),
            pltpu.VMEM((x, x), BF16),
            pltpu.VMEM((slots, 128), F32),
            pltpu.VMEM((slots, 128), F32),
            pltpu.VMEM((slots, x // 2), BF16),
            pltpu.VMEM((slots, x // 2), F32),
            DMA((2, TABLE_CHUNKS)),
            DMA((3,)),
            DMA((2,)),
            DMA((2,)),
            DMA((2,)),
            DMA,
            DMA((2, 4)),
            DMA,
            DMA((CHUNKS,)),
        ],
        compiler_params=pltpu.CompilerParams(
            collective_id=0, has_side_effects=True, vmem_limit_bytes=60 * 1024 * 1024
        ),
    )(
        user_feats[0], tower_in, tower_out, table_a, table_b, ask_rows.reshape(16, 8, 1, CAP),
        slot_src.reshape(slots // 128, 128), slot_req.reshape(slots // 128, 128),
        cross_w, cross_b, head_w,
    )
    live = lax.broadcasted_iota(jnp.int32, (1, 1, slots), 2) < live_counts[0, 0]
    return jnp.where(live, logits.reshape(1, 1, slots), 0.0)


def solution(mesh):
    return jax.shard_map(
        body,
        mesh=mesh,
        in_specs=(
            P("rep", "grp", None), P(), P(),
            P(("grp", "rep"), None), P(("grp", "rep"), None),
            P("grp", "rep", None, None, None), P("grp", "rep", None), P("grp", "rep", None),
            P("rep", "grp"), P(), P(), P(),
        ),
        out_specs=P("grp", "rep", None),
        check_vma=False,
    )
```

```python
import jax
import jax.numpy as jnp
from jax import lax
from jax.experimental import pallas as pl
from jax.experimental.pallas import tpu as pltpu
from jax.sharding import PartitionSpec as P

MESH = pl.DeviceIdType.MESH
DMA = pltpu.SemaphoreType.DMA
BF16 = jnp.bfloat16
F32 = jnp.float32

CAP = 16
STEPS = 128
GROUP = 8
EARLY = 8
PARTS = (0, 32, 64, 112, 128)
CHUNKS = len(PARTS) - 1
TABLE_CHUNKS = 8
TILE = 1024


def remote(src, dst, send, recv, device):
    return pltpu.make_async_remote_copy(
        src_ref=src, dst_ref=dst, send_sem=send, recv_sem=recv, device_id=device, device_id_type=MESH
    )


def dot(a, b):
    return jnp.dot(a, b, preferred_element_type=F32)


def item_places(sources, z, y, x, c):
    owner, k = sources // CAP, sources % CAP
    og, o_r = owner // 8, owner % 8
    dz, dy = (z - og // 4 + 4) % 4, (y - og % 4 + 4) % 4
    dx, dc = (x - o_r // 2 + 4) % 4, (c - o_r % 2 + 2) % 2
    a, b, e = dx, (dy - dx + 4) % 4, (dz - dy + 4) % 4
    return ((e * 16 + b * 4 + a) * 2 + dc) * CAP + k


def request_places(requests, z, y):
    og = requests // 256
    slot = ((z - og // 4 + 4) % 4) * 4 + (y - og % 4 + 4) % 4
    return (requests // 128) % 2 * 2048 + slot * 128 + requests % 128


def to_columns(places, columns):
    wide = places.astype(F32)
    for k in range(places.shape[0]):
        row = jnp.broadcast_to(wide[k : k + 1, :], (128, 128))
        columns[128 * k : 128 * (k + 1), :] = row.T


def onehot(column, first, width):
    lanes = lax.broadcasted_iota(jnp.int32, (1, 128), 1).astype(F32)
    parts = [
        jnp.where(column == lanes + (first + 128 * k), 1.0, 0.0).astype(BF16) for k in range(width // 128)
    ]
    return jnp.concatenate(parts, axis=1)


def ranking_kernel(
    feats_ref, tower_in_ref, tower_out_ref, table_a_ref, table_b_ref, asks_ref, src_ref, req_ref,
    cross_w_ref, cross_b_ref, head_ref, logits_ref,
    src, req, cross_b, head_vmem, tables, stage, ids_half, ids_mine, ids_smem, send_rows, recv_rows, rows_wide, feats_all,
    cross_w, tower_in, tower_out, flipped, src_col, req_col, user, items,
    small_sem, table_sem, weight_sem, local_sem, ids_send, ids_recv, ag_send, ag_recv, row_send, row_recv,
):
    g, r = lax.axis_index("grp"), lax.axis_index("rep")
    z, y, x, c = g // 4, g % 4, r // 2, r % 2
    g_line = [(g + i) % 16 for i in range(16)]
    r_line = [(r + i) % 8 for i in range(8)]
    y_line = [z * 4 + (y + i) % 4 for i in range(4)]
    z_line = [((z + i) % 4) * 4 + y for i in range(4)]

    span = tables.shape[0] // TABLE_CHUNKS
    small_copies = [
        pltpu.make_async_copy(ref, scratch, small_sem.at[n])
        for n, (ref, scratch) in enumerate(
            (
                (feats_ref.at[0, pl.ds(0, 128)], feats_all.at[0]),
                (feats_ref.at[0, pl.ds(128, 128)], feats_all.at[16]),
                (src_ref, src),
                (req_ref, req),
                (cross_b_ref, cross_b),
                (head_ref, head_vmem),
            )
        )
    ]
    for copy in small_copies:
        copy.start()

    barrier = pltpu.get_barrier_semaphore()
    for i in range(1, 8):
        pl.semaphore_signal(barrier, inc=1, device_id=(g, r_line[i]), device_id_type=MESH)
    for i in range(1, 16):
        pl.semaphore_signal(barrier, inc=1, device_id=(g_line[i], r), device_id_type=MESH)

    table_copies = []
    for k in range(TABLE_CHUNKS):
        for t, ref in enumerate((table_a_ref, table_b_ref)):
            table_copies.append(
                pltpu.make_async_copy(
                    ref.at[pl.ds(k * span, span)], stage.at[t, pl.ds(k * span, span)], table_sem.at[t, k]
                )
            )
    for copy in table_copies:
        copy.start()
    weight_copies = [
        pltpu.make_async_copy(ref, scratch, weight_sem.at[n])
        for n, (ref, scratch) in enumerate(
            ((tower_in_ref, tower_in), (tower_out_ref, tower_out), (cross_w_ref, cross_w))
        )
    ]
    for copy in weight_copies:
        copy.start()

    for copy in small_copies:
        copy.wait()
    pl.semaphore_wait(barrier, 22)

    first = [remote(asks_ref.at[:, r_line[i]], ids_half.at[:, r], ids_send.at[0], ids_recv.at[0], (g, r_line[i])) for i in range(1, 8)]
    for copy in first:
        copy.start()
    own = pltpu.make_async_copy(asks_ref.at[:, r], ids_half.at[:, r], local_sem.at[0])
    own.start()
    def block(h, first, second):
        return 4 * second + first if h == 0 else 16 + 4 * first + second

    def hand_on(h, at, to, leg, hop, part=None):
        line = (y_line, z_line)[h if leg == 0 else 1 - h]
        rows = pl.ds(0, 128) if part is None else pl.ds(64 * part, 64)
        a, b = block(h, *at), block(h, *to)
        remote(feats_all.at[a, rows], feats_all.at[b, rows], ag_send, ag_recv.at[b], (line[hop], r)).start()

    def have(h, first, second):
        part = feats_all.at[block(h, first, second)]
        pltpu.make_async_copy(part, part, ag_recv.at[block(h, first, second)]).wait()

    def to_both(h, first):
        for hop in (1, 3):
            hand_on(h, (first, 0), (first, hop), 1, hop)

    for h in range(2):
        for hop in (1, 3):
            hand_on(h, (0, 0), (hop, 0), 0, hop)
    for h in range(2):
        to_both(h, 0)

    for k in range(TABLE_CHUNKS):
        for t in range(2):
            table_copies[2 * k + t].wait()

        @pl.loop(0, span // 64)
        def _(j):
            at = pl.multiple_of(k * span + j * 64, 64)
            tables[pl.ds(at, 64), 0:256] = stage[0, pl.ds(at, 64), :].astype(F32)
            tables[pl.ds(at, 64), 256:512] = stage[1, pl.ds(at, 64), :].astype(F32)

    own.wait()
    pltpu.make_async_copy(ids_half.at[:, pl.ds(0, 7)], ids_half.at[:, pl.ds(0, 7)], ids_recv.at[0]).wait()
    for i in range(1, 16):
        remote(ids_half.at[g_line[i]], ids_mine.at[g], ids_send.at[1], ids_recv.at[1], (g_line[i], r)).start()
    own = pltpu.make_async_copy(ids_half.at[g], ids_mine.at[g], local_sem.at[0])
    own.start()
    for n, hop in enumerate((1, 3)):
        for h in range(2):
            have(h, hop, 0)
            hand_on(h, (hop, 0), (2, 0), 0, hop, n)
            to_both(h, hop)
    for n, hop in enumerate((1, 3)):
        for h in range(2):
            have(h, 0, hop)
            hand_on(h, (0, hop), (0, 2), 1, hop, n)

    slots, half = user.shape
    bias = cross_b[...]
    head = head_vmem[...].astype(F32).reshape(1, 2 * half)
    to_columns(item_places(src[...], z, y, x, c), src_col)
    to_columns(request_places(req[...], z, y), req_col)
    for copy in weight_copies:
        copy.wait()
    flipped[...] = (cross_w[2].astype(F32) * head).T.astype(BF16)

    for h in range(2):
        have(h, 2, 0)
        to_both(h, 2)
    for first in (1, 3):
        for n, hop in enumerate((1, 3)):
            for h in range(2):
                have(h, first, hop)
                hand_on(h, (first, hop), (first, 2), 1, hop, n)

    own.wait()
    pltpu.make_async_copy(ids_half.at[pl.ds(0, 15)], ids_mine.at[pl.ds(0, 15)], ids_recv.at[1]).wait()
    to_smem = pltpu.make_async_copy(ids_mine, ids_smem, local_sem.at[1])
    to_smem.start()
    to_smem.wait()

    r_hops = [((x + hop) % 4) * 2 + (c + dc) % 2 for hop in range(4) for dc in range(2)]

    def partner(j, m):
        hop_y = m // 2 + j % 4
        hop_z = hop_y + j // 4
        return ((z + hop_z) % 4) * 4 + (y + hop_y) % 4, r_hops[m]

    def gather(j):
        for m in range(GROUP):
            to_g, to_r = partner(j, m)
            for k in range(CAP):
                rows_wide[m % 2, pl.ds(k, 1), :] = tables[pl.ds(ids_smem[to_g, to_r, 0, k], 1), :]
            send_rows[j * GROUP + m] = rows_wide[m % 2].astype(BF16)

    def send(j, k, first=0):
        for m in range(first, GROUP):
            i = j * GROUP + m
            remote(send_rows.at[i], recv_rows.at[i], row_send, row_recv.at[k], partner(j, m)).start()

    @pl.loop(0, EARLY)
    def _(j):
        gather(j)

    for n, hop in enumerate((1, 3)):
        for h in range(2):
            have(h, 2, hop)
            hand_on(h, (2, hop), (2, 2), 1, hop, n)

    recv_rows[0] = send_rows[0]
    send(0, 0, 1)
    for k in range(CHUNKS):
        first, last = max(PARTS[k] // GROUP, 1), PARTS[k + 1] // GROUP

        @pl.loop(first, min(max(EARLY, first), last))
        def _(j):
            send(j, k)

        @pl.loop(min(max(EARLY, first), last), last)
        def _(j):
            gather(j)
            send(j, k)

    def arrived(k):
        part = recv_rows.at[pl.ds(max(PARTS[k], 1), PARTS[k + 1] - max(PARTS[k], 1))]
        pltpu.make_async_copy(part, part, row_recv.at[k]).wait()

    def tile(t, first=0):
        return pl.ds(pl.multiple_of(first + t * TILE, TILE), TILE)

    def picked(t, k):
        first, width = PARTS[k] * CAP, (PARTS[k + 1] - PARTS[k]) * CAP
        rows = recv_rows[PARTS[k] : PARTS[k + 1]].reshape(width, half)
        return dot(onehot(src_col[tile(t), :], first, width), rows)

    def pick_part(k):
        arrived(k)

        @pl.loop(0, slots // TILE)
        def _(t):
            items[tile(t), :] = picked(t, k) if k == 0 else items[tile(t), :] + picked(t, k)

    for first in range(4):
        for h in range(2):
            have(h, first, 2)

    @pl.loop(0, slots // TILE)
    def _(t):
        places = onehot(req_col[tile(t), :], 0, 4096)
        user[tile(t), 0:256] = dot(places, feats_all[...].reshape(4096, 256)).astype(BF16)

    @pl.loop(0, slots // TILE)
    def _(t):
        hidden = jnp.maximum(dot(user[tile(t), 0:256], tower_in[...]), 0.0).astype(BF16)
        user[tile(t), :] = dot(hidden, tower_out[...]).astype(BF16)

    @pl.loop(0, slots // TILE)
    def _(t):
        vec = user[tile(t), :]
        for n in range(2):
            cols = slice(half * n, half * (n + 1))
            tables[tile(t, n * slots), :] = dot(vec, cross_w[0, 0:half, cols]) + (bias[0:1, cols] + 1.0)
            tables[tile(t, (n + 2) * slots), :] = dot(vec, flipped[0:half, cols]) + head[:, cols]

    for k in range(CHUNKS - 1):
        pick_part(k)
    arrived(CHUNKS - 1)

    by_bias = head * bias[2:3, :]

    @pl.loop(0, slots // TILE)
    def _(t):
        item = (items[tile(t), :] + picked(t, CHUNKS - 1)).astype(BF16)
        base = (user[tile(t), :], item)
        crossed = []
        for n in range(2):
            cols = slice(half * n, half * (n + 1))
            mixed = dot(item, cross_w[0, half:, cols]) + tables[tile(t, n * slots), :]
            crossed.append((base[n].astype(F32) * mixed).astype(BF16))
        crossed_1 = jnp.concatenate(crossed, axis=1)
        total = jnp.zeros((TILE, 128), F32)
        for n in range(2):
            cols = slice(half * n, half * (n + 1))
            wide = base[n].astype(F32)
            mixed = dot(crossed_1, cross_w[1, :, cols]) + bias[1:2, cols]
            crossed_2 = (wide * mixed + crossed[n].astype(F32)).astype(BF16).astype(F32)
            turned = dot(item, flipped[half:, cols]) + tables[tile(t, (n + 2) * slots), :]
            score = crossed_2 * turned + wide * by_bias[:, cols]
            for m in range(half // 128):
                total += score[:, 128 * m : 128 * (m + 1)]
        for m in range(TILE // 128):
            logits_ref[pl.ds(t * (TILE // 128) + m, 1), :] = jnp.sum(
                total[128 * m : 128 * (m + 1), :].T, axis=0, keepdims=True
            )

    pltpu.make_async_copy(ids_half.at[:, pl.ds(0, 7)], ids_half.at[:, pl.ds(0, 7)], ids_send.at[0]).wait()
    pltpu.make_async_copy(ids_half.at[pl.ds(0, 15)], ids_mine.at[pl.ds(0, 15)], ids_send.at[1]).wait()
    pltpu.make_async_copy(feats_all.at[pl.ds(0, 30)], feats_all.at[pl.ds(0, 30)], ag_send).wait()
    part = send_rows.at[pl.ds(0, STEPS - 1)]
    pltpu.make_async_copy(part, part, row_send).wait()


def body(
    user_feats, tower_in, tower_out, table_a, table_b, ask_rows, slot_src, slot_req, live_counts, cross_w, cross_b, head_w,
):
    vmem = pl.BlockSpec(memory_space=pltpu.VMEM)
    anywhere = pl.BlockSpec(memory_space=pl.ANY)
    rows_dev, e = table_a.shape
    slots = slot_src.shape[-1]
    x = cross_w.shape[-1]
    logits = pl.pallas_call(
        ranking_kernel,
        out_shape=jax.ShapeDtypeStruct((slots // 128, 128), F32),
        in_specs=[anywhere] * 11,
        out_specs=vmem,
        scratch_shapes=[
            pltpu.VMEM((slots // 128, 128), jnp.int32),
            pltpu.VMEM((slots // 128, 128), jnp.int32),
            pltpu.VMEM(cross_b.shape, F32),
            pltpu.VMEM(head_w.shape, BF16),
            pltpu.VMEM((rows_dev, 2 * e), F32),
            pltpu.VMEM((2, rows_dev, e), BF16),
            pltpu.VMEM((16, 8, 1, CAP), jnp.int32),
            pltpu.VMEM((16, 8, 1, CAP), jnp.int32),
            pltpu.SMEM((16, 8, 1, CAP), jnp.int32),
            pltpu.VMEM((STEPS, CAP, 2 * e), BF16),
            pltpu.VMEM((STEPS, CAP, 2 * e), BF16),
            pltpu.VMEM((2, CAP, 2 * e), F32),
            pltpu.VMEM((32, 128, user_feats.shape[-1]), BF16),
            pltpu.VMEM(cross_w.shape, BF16),
            pltpu.VMEM(tower_in.shape, BF16),
            pltpu.VMEM(tower_out.shape, BF16),
            pltpu.VMEM((x, x), BF16),
            pltpu.VMEM((slots, 128), F32),
            pltpu.VMEM((slots, 128), F32),
            pltpu.VMEM((slots, x // 2), BF16),
            pltpu.VMEM((slots, x // 2), F32),
            DMA((6,)),
            DMA((2, TABLE_CHUNKS)),
            DMA((3,)),
            DMA((2,)),
            DMA((2,)),
            DMA((2,)),
            DMA,
            DMA((32,)),
            DMA,
            DMA((CHUNKS,)),
        ],
        compiler_params=pltpu.CompilerParams(
            collective_id=0, has_side_effects=True, vmem_limit_bytes=60 * 1024 * 1024
        ),
    )(
        user_feats, tower_in, tower_out, table_a, table_b, ask_rows.reshape(16, 8, 1, CAP),
        slot_src.reshape(slots // 128, 128), slot_req.reshape(slots // 128, 128),
        cross_w, cross_b, head_w,
    )
    live = lax.broadcasted_iota(jnp.int32, (1, 1, slots), 2) < live_counts[0, 0]
    return jnp.where(live, logits.reshape(1, 1, slots), 0.0)


def solution(mesh):
    return jax.shard_map(
        body,
        mesh=mesh,
        in_specs=(
            P("rep", "grp", None), P(), P(),
            P(("grp", "rep"), None), P(("grp", "rep"), None),
            P("grp", "rep", None, None, None), P("grp", "rep", None), P("grp", "rep", None),
            P("rep", "grp"), P(), P(), P(),
        ),
        out_specs=P("grp", "rep", None),
        check_vma=False,
    )
```

```python
import jax
import jax.numpy as jnp
from jax import lax
from jax.experimental import pallas as pl
from jax.experimental.pallas import tpu as pltpu
from jax.sharding import PartitionSpec as P

MESH = pl.DeviceIdType.MESH
DMA = pltpu.SemaphoreType.DMA
BF16 = jnp.bfloat16
F32 = jnp.float32

CAP = 16
STEPS = 128
GROUP = 8
EARLY = 3
PARTS = (0, 48, 96, 112, 128)
CHUNKS = len(PARTS) - 1
TABLE_CHUNKS = 8
TILE = 1024


def remote(src, dst, send, recv, device):
    return pltpu.make_async_remote_copy(
        src_ref=src, dst_ref=dst, send_sem=send, recv_sem=recv, device_id=device, device_id_type=MESH
    )


def dot(a, b):
    return jnp.dot(a, b, preferred_element_type=F32)


def item_places(sources, z, y, x, c):
    owner, k = sources // CAP, sources % CAP
    og, o_r = owner // 8, owner % 8
    dz, dy = (z - og // 4 + 4) % 4, (y - og % 4 + 4) % 4
    dx, dc = (x - o_r // 2 + 4) % 4, (c - o_r % 2 + 2) % 2
    a, b, e = dx, (dy - dx + 4) % 4, (dz - dy + 4) % 4
    return ((e * 16 + b * 4 + a) * 2 + dc) * CAP + k


def request_places(requests, z, y):
    og = requests // 256
    slot = ((z - og // 4 + 4) % 4) * 4 + (y - og % 4 + 4) % 4
    return (requests // 128) % 2 * 2048 + slot * 128 + requests % 128


def to_columns(places, columns):
    wide = places.astype(F32)
    for k in range(places.shape[0]):
        row = jnp.broadcast_to(wide[k : k + 1, :], (128, 128))
        columns[128 * k : 128 * (k + 1), :] = row.T


def onehot(column, first, width):
    lanes = lax.broadcasted_iota(jnp.int32, (1, 128), 1).astype(F32)
    parts = [
        jnp.where(column == lanes + (first + 128 * k), 1.0, 0.0).astype(BF16) for k in range(width // 128)
    ]
    return jnp.concatenate(parts, axis=1)


def ranking_kernel(
    feats_ref, tower_in_ref, tower_out_ref, table_a_ref, table_b_ref, asks_ref, src_ref, req_ref,
    cross_w_ref, cross_b_ref, head_ref, logits_ref,
    src, req, cross_b, head_vmem, tables, stage, ids_half, ids_mine, ids_smem, send_rows, recv_rows, rows_wide, feats_all,
    cross_w, tower_in, tower_out, flipped, src_col, req_col, user, items,
    small_sem, table_sem, weight_sem, local_sem, ids_send, ids_recv, ag_send, ag_recv, row_send, row_recv,
):
    g, r = lax.axis_index("grp"), lax.axis_index("rep")
    z, y, x, c = g // 4, g % 4, r // 2, r % 2
    g_line = [(g + i) % 16 for i in range(16)]
    r_line = [(r + i) % 8 for i in range(8)]
    y_line = [z * 4 + (y + i) % 4 for i in range(4)]
    z_line = [((z + i) % 4) * 4 + y for i in range(4)]

    span = tables.shape[0] // TABLE_CHUNKS
    small_copies = [
        pltpu.make_async_copy(ref, scratch, small_sem.at[n])
        for n, (ref, scratch) in enumerate(
            (
                (feats_ref.at[0, pl.ds(0, 128)], feats_all.at[0]),
                (feats_ref.at[0, pl.ds(128, 128)], feats_all.at[16]),
                (src_ref, src),
                (req_ref, req),
                (cross_b_ref, cross_b),
                (head_ref, head_vmem),
            )
        )
    ]
    for copy in small_copies:
        copy.start()

    barrier = pltpu.get_barrier_semaphore()
    for i in range(1, 8):
        pl.semaphore_signal(barrier, inc=1, device_id=(g, r_line[i]), device_id_type=MESH)
    for i in range(1, 16):
        pl.semaphore_signal(barrier, inc=1, device_id=(g_line[i], r), device_id_type=MESH)

    table_copies = []
    for k in range(TABLE_CHUNKS):
        for t, ref in enumerate((table_a_ref, table_b_ref)):
            table_copies.append(
                pltpu.make_async_copy(
                    ref.at[pl.ds(k * span, span)], stage.at[t, pl.ds(k * span, span)], table_sem.at[t, k]
                )
            )
    for copy in table_copies:
        copy.start()
    weight_copies = [
        pltpu.make_async_copy(ref, scratch, weight_sem.at[n])
        for n, (ref, scratch) in enumerate(
            ((tower_in_ref, tower_in), (tower_out_ref, tower_out), (cross_w_ref, cross_w))
        )
    ]
    for copy in weight_copies:
        copy.start()

    for copy in small_copies:
        copy.wait()
    pl.semaphore_wait(barrier, 22)

    first = [remote(asks_ref.at[:, r_line[i]], ids_half.at[:, r], ids_send.at[0], ids_recv.at[0], (g, r_line[i])) for i in range(1, 8)]
    for copy in first:
        copy.start()
    own = pltpu.make_async_copy(asks_ref.at[:, r], ids_half.at[:, r], local_sem.at[0])
    own.start()
    def block(h, first, second):
        return 4 * second + first if h == 0 else 16 + 4 * first + second

    def hand_on(h, at, to, leg, hop, part=None):
        line = (y_line, z_line)[h if leg == 0 else 1 - h]
        rows = pl.ds(0, 128) if part is None else pl.ds(64 * part, 64)
        a, b = block(h, *at), block(h, *to)
        remote(feats_all.at[a, rows], feats_all.at[b, rows], ag_send, ag_recv.at[b], (line[hop], r)).start()

    def have(h, first, second):
        part = feats_all.at[block(h, first, second)]
        pltpu.make_async_copy(part, part, ag_recv.at[block(h, first, second)]).wait()

    def to_both(h, first):
        for hop in (1, 3):
            hand_on(h, (first, 0), (first, hop), 1, hop)

    for h in range(2):
        for hop in (1, 3):
            hand_on(h, (0, 0), (hop, 0), 0, hop)
    for h in range(2):
        to_both(h, 0)

    for k in range(TABLE_CHUNKS):
        for t in range(2):
            table_copies[2 * k + t].wait()

        @pl.loop(0, span // 64)
        def _(j):
            at = pl.multiple_of(k * span + j * 64, 64)
            tables[pl.ds(at, 64), 0:256] = stage[0, pl.ds(at, 64), :].astype(F32)
            tables[pl.ds(at, 64), 256:512] = stage[1, pl.ds(at, 64), :].astype(F32)

    own.wait()
    pltpu.make_async_copy(ids_half.at[:, pl.ds(0, 7)], ids_half.at[:, pl.ds(0, 7)], ids_recv.at[0]).wait()
    for i in range(1, 16):
        remote(ids_half.at[g_line[i]], ids_mine.at[g], ids_send.at[1], ids_recv.at[1], (g_line[i], r)).start()
    own = pltpu.make_async_copy(ids_half.at[g], ids_mine.at[g], local_sem.at[0])
    own.start()
    for n, hop in enumerate((1, 3)):
        for h in range(2):
            have(h, hop, 0)
            hand_on(h, (hop, 0), (2, 0), 0, hop, n)
            to_both(h, hop)
    for n, hop in enumerate((1, 3)):
        for h in range(2):
            have(h, 0, hop)
            hand_on(h, (0, hop), (0, 2), 1, hop, n)

    slots, half = user.shape
    bias = cross_b[...]
    head = head_vmem[...].astype(F32).reshape(1, 2 * half)
    to_columns(item_places(src[...], z, y, x, c), src_col)
    to_columns(request_places(req[...], z, y), req_col)

    for h in range(2):
        have(h, 2, 0)
        to_both(h, 2)
    for first in (1, 3):
        for n, hop in enumerate((1, 3)):
            for h in range(2):
                have(h, first, hop)
                hand_on(h, (first, hop), (first, 2), 1, hop, n)

    own.wait()
    pltpu.make_async_copy(ids_half.at[pl.ds(0, 15)], ids_mine.at[pl.ds(0, 15)], ids_recv.at[1]).wait()
    to_smem = pltpu.make_async_copy(ids_mine, ids_smem, local_sem.at[1])
    to_smem.start()
    to_smem.wait()

    r_hops = [((x + hop) % 4) * 2 + (c + dc) % 2 for hop in range(4) for dc in range(2)]

    def partner(j, m):
        hop_y = m // 2 + j % 4
        hop_z = hop_y + j // 4
        return ((z + hop_z) % 4) * 4 + (y + hop_y) % 4, r_hops[m]

    def gather(j):
        for m in range(GROUP):
            to_g, to_r = partner(j, m)
            for k in range(CAP):
                rows_wide[m % 2, pl.ds(k, 1), :] = tables[pl.ds(ids_smem[to_g, to_r, 0, k], 1), :]
            send_rows[j * GROUP + m] = rows_wide[m % 2].astype(BF16)

    def send(j, k, first=0):
        for m in range(first, GROUP):
            i = j * GROUP + m
            remote(send_rows.at[i], recv_rows.at[i], row_send, row_recv.at[k], partner(j, m)).start()

    @pl.loop(0, 1)
    def _(j):
        gather(j)

    for n, hop in enumerate((1, 3)):
        for h in range(2):
            have(h, 2, hop)
            hand_on(h, (2, hop), (2, 2), 1, hop, n)

    @pl.loop(1, EARLY)
    def _(j):
        gather(j)

    for first in (0, 1, 3):
        for h in range(2):
            have(h, first, 2)

    recv_rows[0] = send_rows[0]
    send(0, 0, 1)
    for k in range(CHUNKS):
        first, last = max(PARTS[k] // GROUP, 1), PARTS[k + 1] // GROUP

        @pl.loop(first, min(max(EARLY, first), last))
        def _(j):
            send(j, k)

        @pl.loop(min(max(EARLY, first), last), last)
        def _(j):
            gather(j)
            send(j, k)

    def arrived(k):
        part = recv_rows.at[pl.ds(max(PARTS[k], 1), PARTS[k + 1] - max(PARTS[k], 1))]
        pltpu.make_async_copy(part, part, row_recv.at[k]).wait()

    def tile(t, first=0):
        return pl.ds(pl.multiple_of(first + t * TILE, TILE), TILE)

    def picked(t, k):
        first, width = PARTS[k] * CAP, (PARTS[k + 1] - PARTS[k]) * CAP
        rows = recv_rows[PARTS[k] : PARTS[k + 1]].reshape(width, half)
        return dot(onehot(src_col[tile(t), :], first, width), rows)

    def pick_part(k):
        arrived(k)

        @pl.loop(0, slots // TILE)
        def _(t):
            items[tile(t), :] = picked(t, k) if k == 0 else items[tile(t), :] + picked(t, k)

    for copy in weight_copies:
        copy.wait()
    flipped[...] = (cross_w[2].astype(F32) * head).T.astype(BF16)

    for h in range(2):
        have(h, 2, 2)

    @pl.loop(0, slots // TILE)
    def _(t):
        places = onehot(req_col[tile(t), :], 0, 4096)
        user[tile(t), 0:256] = dot(places, feats_all[...].reshape(4096, 256)).astype(BF16)

    @pl.loop(0, slots // TILE)
    def _(t):
        hidden = jnp.maximum(dot(user[tile(t), 0:256], tower_in[...]), 0.0).astype(BF16)
        user[tile(t), :] = dot(hidden, tower_out[...]).astype(BF16)

    @pl.loop(0, slots // TILE)
    def _(t):
        vec = user[tile(t), :]
        for n in range(2):
            cols = slice(half * n, half * (n + 1))
            tables[tile(t, n * slots), :] = dot(vec, cross_w[0, 0:half, cols]) + (bias[0:1, cols] + 1.0)
            tables[tile(t, (n + 2) * slots), :] = dot(vec, flipped[0:half, cols]) + head[:, cols]

    for k in range(CHUNKS - 1):
        pick_part(k)
    arrived(CHUNKS - 1)

    by_bias = head * bias[2:3, :]

    @pl.loop(0, slots // TILE)
    def _(t):
        item = (items[tile(t), :] + picked(t, CHUNKS - 1)).astype(BF16)
        base = (user[tile(t), :], item)
        crossed = []
        for n in range(2):
            cols = slice(half * n, half * (n + 1))
            mixed = dot(item, cross_w[0, half:, cols]) + tables[tile(t, n * slots), :]
            crossed.append((base[n].astype(F32) * mixed).astype(BF16))
        crossed_1 = jnp.concatenate(crossed, axis=1)
        total = jnp.zeros((TILE, 128), F32)
        for n in range(2):
            cols = slice(half * n, half * (n + 1))
            wide = base[n].astype(F32)
            mixed = dot(crossed_1, cross_w[1, :, cols]) + bias[1:2, cols]
            crossed_2 = (wide * mixed + crossed[n].astype(F32)).astype(BF16).astype(F32)
            turned = dot(item, flipped[half:, cols]) + tables[tile(t, (n + 2) * slots), :]
            score = crossed_2 * turned + wide * by_bias[:, cols]
            for m in range(half // 128):
                total += score[:, 128 * m : 128 * (m + 1)]
        for m in range(TILE // 128):
            logits_ref[pl.ds(t * (TILE // 128) + m, 1), :] = jnp.sum(
                total[128 * m : 128 * (m + 1), :].T, axis=0, keepdims=True
            )

    pltpu.make_async_copy(ids_half.at[:, pl.ds(0, 7)], ids_half.at[:, pl.ds(0, 7)], ids_send.at[0]).wait()
    pltpu.make_async_copy(ids_half.at[pl.ds(0, 15)], ids_mine.at[pl.ds(0, 15)], ids_send.at[1]).wait()
    pltpu.make_async_copy(feats_all.at[pl.ds(0, 30)], feats_all.at[pl.ds(0, 30)], ag_send).wait()
    part = send_rows.at[pl.ds(0, STEPS - 1)]
    pltpu.make_async_copy(part, part, row_send).wait()


def body(
    user_feats, tower_in, tower_out, table_a, table_b, ask_rows, slot_src, slot_req, live_counts, cross_w, cross_b, head_w,
):
    vmem = pl.BlockSpec(memory_space=pltpu.VMEM)
    anywhere = pl.BlockSpec(memory_space=pl.ANY)
    rows_dev, e = table_a.shape
    slots = slot_src.shape[-1]
    x = cross_w.shape[-1]
    logits = pl.pallas_call(
        ranking_kernel,
        out_shape=jax.ShapeDtypeStruct((slots // 128, 128), F32),
        in_specs=[anywhere] * 11,
        out_specs=vmem,
        scratch_shapes=[
            pltpu.VMEM((slots // 128, 128), jnp.int32),
            pltpu.VMEM((slots // 128, 128), jnp.int32),
            pltpu.VMEM(cross_b.shape, F32),
            pltpu.VMEM(head_w.shape, BF16),
            pltpu.VMEM((rows_dev, 2 * e), F32),
            pltpu.VMEM((2, rows_dev, e), BF16),
            pltpu.VMEM((16, 8, 1, CAP), jnp.int32),
            pltpu.VMEM((16, 8, 1, CAP), jnp.int32),
            pltpu.SMEM((16, 8, 1, CAP), jnp.int32),
            pltpu.VMEM((STEPS, CAP, 2 * e), BF16),
            pltpu.VMEM((STEPS, CAP, 2 * e), BF16),
            pltpu.VMEM((2, CAP, 2 * e), F32),
            pltpu.VMEM((32, 128, user_feats.shape[-1]), BF16),
            pltpu.VMEM(cross_w.shape, BF16),
            pltpu.VMEM(tower_in.shape, BF16),
            pltpu.VMEM(tower_out.shape, BF16),
            pltpu.VMEM((x, x), BF16),
            pltpu.VMEM((slots, 128), F32),
            pltpu.VMEM((slots, 128), F32),
            pltpu.VMEM((slots, x // 2), BF16),
            pltpu.VMEM((slots, x // 2), F32),
            DMA((6,)),
            DMA((2, TABLE_CHUNKS)),
            DMA((3,)),
            DMA((2,)),
            DMA((2,)),
            DMA((2,)),
            DMA,
            DMA((32,)),
            DMA,
            DMA((CHUNKS,)),
        ],
        compiler_params=pltpu.CompilerParams(
            collective_id=0, has_side_effects=True, vmem_limit_bytes=60 * 1024 * 1024
        ),
    )(
        user_feats, tower_in, tower_out, table_a, table_b, ask_rows.reshape(16, 8, 1, CAP),
        slot_src.reshape(slots // 128, 128), slot_req.reshape(slots // 128, 128),
        cross_w, cross_b, head_w,
    )
    live = lax.broadcasted_iota(jnp.int32, (1, 1, slots), 2) < live_counts[0, 0]
    return jnp.where(live, logits.reshape(1, 1, slots), 0.0)


def solution(mesh):
    return jax.shard_map(
        body,
        mesh=mesh,
        in_specs=(
            P("rep", "grp", None), P(), P(),
            P(("grp", "rep"), None), P(("grp", "rep"), None),
            P("grp", "rep", None, None, None), P("grp", "rep", None), P("grp", "rep", None),
            P("rep", "grp"), P(), P(), P(),
        ),
        out_specs=P("grp", "rep", None),
        check_vma=False,
    )
```

```python
import jax
import jax.numpy as jnp
from jax import lax
from jax.experimental import pallas as pl
from jax.experimental.pallas import tpu as pltpu
from jax.sharding import PartitionSpec as P

MESH = pl.DeviceIdType.MESH
DMA = pltpu.SemaphoreType.DMA
BF16 = jnp.bfloat16
F32 = jnp.float32

CAP = 16
STEPS = 128
GROUP = 8
EARLY = 3
PARTS = (0, 80, 112, 128)
CHUNKS = len(PARTS) - 1
TABLE_CHUNKS = 8
TILE = 1024


def remote(src, dst, send, recv, device):
    return pltpu.make_async_remote_copy(
        src_ref=src, dst_ref=dst, send_sem=send, recv_sem=recv, device_id=device, device_id_type=MESH
    )


def dot(a, b):
    return jnp.dot(a, b, preferred_element_type=F32)


def item_places(sources, z, y, x, c):
    owner, k = sources // CAP, sources % CAP
    og, o_r = owner // 8, owner % 8
    dz, dy = (z - og // 4 + 4) % 4, (y - og % 4 + 4) % 4
    dx, dc = (x - o_r // 2 + 4) % 4, (c - o_r % 2 + 2) % 2
    a, b, e = dx, (dy - dx + 4) % 4, (dz - dy + 4) % 4
    return ((e * 16 + b * 4 + a) * 2 + dc) * CAP + k


def request_places(requests, z, y):
    og = requests // 256
    slot = ((z - og // 4 + 4) % 4) * 4 + (y - og % 4 + 4) % 4
    return (requests // 128) % 2 * 2048 + slot * 128 + requests % 128


def to_columns(places, columns):
    wide = places.astype(F32)
    for k in range(places.shape[0]):
        row = jnp.broadcast_to(wide[k : k + 1, :], (128, 128))
        columns[128 * k : 128 * (k + 1), :] = row.T


def onehot(column, first, width):
    lanes = lax.broadcasted_iota(jnp.int32, (1, 128), 1).astype(F32)
    parts = [
        jnp.where(column == lanes + (first + 128 * k), 1.0, 0.0).astype(BF16) for k in range(width // 128)
    ]
    return jnp.concatenate(parts, axis=1)


def ranking_kernel(
    feats_ref, tower_in_ref, tower_out_ref, table_a_ref, table_b_ref, asks_ref, src_ref, req_ref,
    cross_w_ref, cross_b_ref, head_ref, logits_ref,
    src, req, cross_b, head_vmem, tables, stage, ids_half, ids_mine, ids_smem, send_rows, recv_rows, rows_wide, feats_all,
    cross_w, tower_in, tower_out, flipped, src_col, req_smem, user, rows_a, items,
    small_sem, table_sem, weight_sem, local_sem, ids_send, ids_recv, ag_send, ag_recv, row_send, row_recv,
):
    g, r = lax.axis_index("grp"), lax.axis_index("rep")
    z, y, x, c = g // 4, g % 4, r // 2, r % 2
    g_line = [(g + i) % 16 for i in range(16)]
    r_line = [(r + i) % 8 for i in range(8)]
    y_line = [z * 4 + (y + i) % 4 for i in range(4)]
    z_line = [((z + i) % 4) * 4 + y for i in range(4)]

    span = tables.shape[0] // TABLE_CHUNKS
    small_copies = [
        pltpu.make_async_copy(ref, scratch, small_sem.at[n])
        for n, (ref, scratch) in enumerate(
            (
                (feats_ref.at[0, pl.ds(0, 128)], feats_all.at[0]),
                (feats_ref.at[0, pl.ds(128, 128)], feats_all.at[16]),
                (src_ref, src),
                (req_ref, req),
                (cross_b_ref, cross_b),
                (head_ref, head_vmem),
            )
        )
    ]
    for copy in small_copies:
        copy.start()

    barrier = pltpu.get_barrier_semaphore()
    for i in range(1, 8):
        pl.semaphore_signal(barrier, inc=1, device_id=(g, r_line[i]), device_id_type=MESH)
    for i in range(1, 16):
        pl.semaphore_signal(barrier, inc=1, device_id=(g_line[i], r), device_id_type=MESH)

    table_copies = []
    for k in range(TABLE_CHUNKS):
        for t, ref in enumerate((table_a_ref, table_b_ref)):
            table_copies.append(
                pltpu.make_async_copy(
                    ref.at[pl.ds(k * span, span)], stage.at[t, pl.ds(k * span, span)], table_sem.at[t, k]
                )
            )
    for copy in table_copies:
        copy.start()
    weight_copies = [
        pltpu.make_async_copy(ref, scratch, weight_sem.at[n])
        for n, (ref, scratch) in enumerate(
            ((tower_in_ref, tower_in), (tower_out_ref, tower_out), (cross_w_ref, cross_w))
        )
    ]
    for copy in weight_copies:
        copy.start()

    for copy in small_copies:
        copy.wait()
    pl.semaphore_wait(barrier, 22)

    first = [remote(asks_ref.at[:, r_line[i]], ids_half.at[:, r], ids_send.at[0], ids_recv.at[0], (g, r_line[i])) for i in range(1, 8)]
    for copy in first:
        copy.start()
    own = pltpu.make_async_copy(asks_ref.at[:, r], ids_half.at[:, r], local_sem.at[0])
    own.start()
    def block(h, first, second):
        return 4 * second + first if h == 0 else 16 + 4 * first + second

    def hand_on(h, at, to, leg, hop, part=None):
        line = (y_line, z_line)[h if leg == 0 else 1 - h]
        rows = pl.ds(0, 128) if part is None else pl.ds(64 * part, 64)
        a, b = block(h, *at), block(h, *to)
        remote(feats_all.at[a, rows], feats_all.at[b, rows], ag_send, ag_recv.at[b], (line[hop], r)).start()

    def have(h, first, second):
        part = feats_all.at[block(h, first, second)]
        pltpu.make_async_copy(part, part, ag_recv.at[block(h, first, second)]).wait()

    def to_both(h, first):
        for hop in (1, 3):
            hand_on(h, (first, 0), (first, hop), 1, hop)

    for h in range(2):
        for hop in (1, 3):
            hand_on(h, (0, 0), (hop, 0), 0, hop)
    for h in range(2):
        to_both(h, 0)

    for k in range(TABLE_CHUNKS):
        for t in range(2):
            table_copies[2 * k + t].wait()

        @pl.loop(0, span // 64)
        def _(j):
            at = pl.multiple_of(k * span + j * 64, 64)
            tables[pl.ds(at, 64), 0:256] = stage[0, pl.ds(at, 64), :].astype(F32)
            tables[pl.ds(at, 64), 256:512] = stage[1, pl.ds(at, 64), :].astype(F32)

    own.wait()
    pltpu.make_async_copy(ids_half.at[:, pl.ds(0, 7)], ids_half.at[:, pl.ds(0, 7)], ids_recv.at[0]).wait()
    for i in range(1, 16):
        remote(ids_half.at[g_line[i]], ids_mine.at[g], ids_send.at[1], ids_recv.at[1], (g_line[i], r)).start()
    own = pltpu.make_async_copy(ids_half.at[g], ids_mine.at[g], local_sem.at[0])
    own.start()
    for n, hop in enumerate((1, 3)):
        for h in range(2):
            have(h, hop, 0)
            hand_on(h, (hop, 0), (2, 0), 0, hop, n)
            to_both(h, hop)
    for n, hop in enumerate((1, 3)):
        for h in range(2):
            have(h, 0, hop)
            hand_on(h, (0, hop), (0, 2), 1, hop, n)

    slots, half = user.shape
    width = half // 2
    bias = cross_b[...]
    head = head_vmem[...].astype(F32).reshape(1, 2 * half)
    req[...] = request_places(req[...], z, y)
    to_smem = pltpu.make_async_copy(req, req_smem, local_sem.at[1])
    to_smem.start()
    to_columns(item_places(src[...], z, y, x, c), src_col)
    to_smem.wait()

    for h in range(2):
        have(h, 2, 0)
        to_both(h, 2)
    for first in (1, 3):
        for n, hop in enumerate((1, 3)):
            for h in range(2):
                have(h, first, hop)
                hand_on(h, (first, hop), (first, 2), 1, hop, n)

    own.wait()
    pltpu.make_async_copy(ids_half.at[pl.ds(0, 15)], ids_mine.at[pl.ds(0, 15)], ids_recv.at[1]).wait()
    to_smem = pltpu.make_async_copy(ids_mine, ids_smem, local_sem.at[1])
    to_smem.start()
    to_smem.wait()

    r_hops = [((x + hop) % 4) * 2 + (c + dc) % 2 for hop in range(4) for dc in range(2)]

    def partner(j, m):
        hop_y = m // 2 + j % 4
        hop_z = hop_y + j // 4
        return ((z + hop_z) % 4) * 4 + (y + hop_y) % 4, r_hops[m]

    def gather(j):
        for m in range(GROUP):
            to_g, to_r = partner(j, m)
            for k in range(CAP):
                rows_wide[m, pl.ds(k, 1), :] = tables[pl.ds(ids_smem[to_g, to_r, 0, k], 1), :]
            send_rows[j * GROUP + m] = rows_wide[m].astype(BF16)

    def send(j, n, sem, first=0):
        for m in range(first, GROUP):
            i = j * GROUP + m
            columns = pl.ds(n * width, width)
            remote(
                send_rows.at[i, :, columns], recv_rows.at[i, :, columns], row_send, row_recv.at[sem], partner(j, m)
            ).start()

    @pl.loop(0, 1)
    def _(j):
        gather(j)

    for n, hop in enumerate((1, 3)):
        for h in range(2):
            have(h, 2, hop)
            hand_on(h, (2, hop), (2, 2), 1, hop, n)

    @pl.loop(1, EARLY)
    def _(j):
        gather(j)

    for first in (0, 1, 3):
        for h in range(2):
            have(h, first, 2)

    recv_rows[0] = send_rows[0]
    send(0, 0, CHUNKS, 1)

    @pl.loop(1, EARLY)
    def _(j):
        send(j, 0, CHUNKS)

    @pl.loop(EARLY, STEPS // GROUP)
    def _(j):
        gather(j)
        send(j, 0, CHUNKS)

    def arrived(first, last, columns, sem):
        part = recv_rows.at[pl.ds(max(first, 1), last - max(first, 1)), :, columns]
        pltpu.make_async_copy(part, part, row_recv.at[sem]).wait()

    def tile(t, first=0):
        return pl.ds(pl.multiple_of(first + t * TILE, TILE), TILE)

    def picked(t, k):
        first, count = PARTS[k] * CAP, (PARTS[k + 1] - PARTS[k]) * CAP
        rows = recv_rows[PARTS[k] : PARTS[k + 1], :, width:].reshape(count, width)
        return dot(onehot(src_col[tile(t), :], first, count), rows)

    def pick_part(k):
        arrived(PARTS[k], PARTS[k + 1], pl.ds(width, width), k)

        @pl.loop(0, slots // TILE)
        def _(t):
            items[tile(t), :] = picked(t, k) if k == 0 else items[tile(t), :] + picked(t, k)

    for copy in weight_copies:
        copy.wait()
    flipped[...] = (cross_w[2].astype(F32) * head).T.astype(BF16)

    for h in range(2):
        have(h, 2, 2)

    e = width

    @pl.loop(0, 32)
    def _(j):
        tables[pl.ds(pl.multiple_of(128 * j, 128), 128), 0:e] = feats_all[j].astype(F32)

    @pl.loop(0, slots // 128)
    def _(j):
        for m in range(8):
            for k in range(16):
                rows_wide[m, pl.ds(k, 1), 0:e] = tables[pl.ds(req_smem[j, 16 * m + k], 1), 0:e]
            user[pl.ds(pl.multiple_of(128 * j, 128) + 16 * m, 16), 0:e] = rows_wide[m, :, 0:e].astype(BF16)

    @pl.loop(0, slots // TILE)
    def _(t):
        hidden = jnp.maximum(dot(user[tile(t), 0:256], tower_in[...]), 0.0).astype(BF16)
        user[tile(t), :] = dot(hidden, tower_out[...]).astype(BF16)

    send(0, 1, 0, 1)
    for k in range(CHUNKS):

        @pl.loop(max(PARTS[k] // GROUP, 1), PARTS[k + 1] // GROUP)
        def _(j):
            send(j, 1, k)

    arrived(0, STEPS, pl.ds(0, width), CHUNKS)

    @pl.loop(0, slots // TILE)
    def _(t):
        rows = recv_rows[:, :, 0:width].reshape(STEPS * CAP, width)
        rows_a[tile(t), :] = dot(onehot(src_col[tile(t), :], 0, STEPS * CAP), rows).astype(BF16)

    @pl.loop(0, slots // TILE)
    def _(t):
        early = jnp.concatenate([user[tile(t), :], rows_a[tile(t), :]], axis=1)
        for n in range(2):
            cols = slice(half * n, half * (n + 1))
            tables[tile(t, n * slots), :] = dot(early, cross_w[0, 0 : half + width, cols]) + (bias[0:1, cols] + 1.0)
            tables[tile(t, (n + 2) * slots), :] = dot(early, flipped[0 : half + width, cols]) + head[:, cols]

    for k in range(CHUNKS - 1):
        pick_part(k)
    arrived(PARTS[-2], STEPS, pl.ds(width, width), CHUNKS - 1)

    by_bias = head * bias[2:3, :]

    @pl.loop(0, slots // TILE)
    def _(t):
        item = (items[tile(t), :] + picked(t, CHUNKS - 1)).astype(BF16)
        base = (user[tile(t), :], jnp.concatenate([rows_a[tile(t), :], item], axis=1))
        crossed = []
        for n in range(2):
            cols = slice(half * n, half * (n + 1))
            mixed = dot(item, cross_w[0, half + width :, cols]) + tables[tile(t, n * slots), :]
            crossed.append((base[n].astype(F32) * mixed).astype(BF16))
        crossed_1 = jnp.concatenate(crossed, axis=1)
        total = jnp.zeros((TILE, 128), F32)
        for n in range(2):
            cols = slice(half * n, half * (n + 1))
            wide = base[n].astype(F32)
            mixed = dot(crossed_1, cross_w[1, :, cols]) + bias[1:2, cols]
            crossed_2 = (wide * mixed + crossed[n].astype(F32)).astype(BF16).astype(F32)
            turned = dot(item, flipped[half + width :, cols]) + tables[tile(t, (n + 2) * slots), :]
            score = crossed_2 * turned + wide * by_bias[:, cols]
            for m in range(half // 128):
                total += score[:, 128 * m : 128 * (m + 1)]
        for m in range(TILE // 128):
            logits_ref[pl.ds(t * (TILE // 128) + m, 1), :] = jnp.sum(
                total[128 * m : 128 * (m + 1), :].T, axis=0, keepdims=True
            )

    pltpu.make_async_copy(ids_half.at[:, pl.ds(0, 7)], ids_half.at[:, pl.ds(0, 7)], ids_send.at[0]).wait()
    pltpu.make_async_copy(ids_half.at[pl.ds(0, 15)], ids_mine.at[pl.ds(0, 15)], ids_send.at[1]).wait()
    pltpu.make_async_copy(feats_all.at[pl.ds(0, 30)], feats_all.at[pl.ds(0, 30)], ag_send).wait()
    part = send_rows.at[pl.ds(0, STEPS - 1)]
    pltpu.make_async_copy(part, part, row_send).wait()


def body(
    user_feats, tower_in, tower_out, table_a, table_b, ask_rows, slot_src, slot_req, live_counts, cross_w, cross_b, head_w,
):
    vmem = pl.BlockSpec(memory_space=pltpu.VMEM)
    anywhere = pl.BlockSpec(memory_space=pl.ANY)
    rows_dev, e = table_a.shape
    slots = slot_src.shape[-1]
    x = cross_w.shape[-1]
    logits = pl.pallas_call(
        ranking_kernel,
        out_shape=jax.ShapeDtypeStruct((slots // 128, 128), F32),
        in_specs=[anywhere] * 11,
        out_specs=vmem,
        scratch_shapes=[
            pltpu.VMEM((slots // 128, 128), jnp.int32),
            pltpu.VMEM((slots // 128, 128), jnp.int32),
            pltpu.VMEM(cross_b.shape, F32),
            pltpu.VMEM(head_w.shape, BF16),
            pltpu.VMEM((rows_dev, 2 * e), F32),
            pltpu.VMEM((2, rows_dev, e), BF16),
            pltpu.VMEM((16, 8, 1, CAP), jnp.int32),
            pltpu.VMEM((16, 8, 1, CAP), jnp.int32),
            pltpu.SMEM((16, 8, 1, CAP), jnp.int32),
            pltpu.VMEM((STEPS, CAP, 2 * e), BF16),
            pltpu.VMEM((STEPS, CAP, 2 * e), BF16),
            pltpu.VMEM((GROUP, CAP, 2 * e), F32),
            pltpu.VMEM((32, 128, user_feats.shape[-1]), BF16),
            pltpu.VMEM(cross_w.shape, BF16),
            pltpu.VMEM(tower_in.shape, BF16),
            pltpu.VMEM(tower_out.shape, BF16),
            pltpu.VMEM((x, x), BF16),
            pltpu.VMEM((slots, 128), F32),
            pltpu.SMEM((slots // 128, 128), jnp.int32),
            pltpu.VMEM((slots, x // 2), BF16),
            pltpu.VMEM((slots, e), BF16),
            pltpu.VMEM((slots, e), F32),
            DMA((6,)),
            DMA((2, TABLE_CHUNKS)),
            DMA((3,)),
            DMA((2,)),
            DMA((2,)),
            DMA((2,)),
            DMA,
            DMA((32,)),
            DMA,
            DMA((CHUNKS + 1,)),
        ],
        compiler_params=pltpu.CompilerParams(
            collective_id=0, has_side_effects=True, vmem_limit_bytes=60 * 1024 * 1024
        ),
    )(
        user_feats, tower_in, tower_out, table_a, table_b, ask_rows.reshape(16, 8, 1, CAP),
        slot_src.reshape(slots // 128, 128), slot_req.reshape(slots // 128, 128),
        cross_w, cross_b, head_w,
    )
    live = lax.broadcasted_iota(jnp.int32, (1, 1, slots), 2) < live_counts[0, 0]
    return jnp.where(live, logits.reshape(1, 1, slots), 0.0)


def solution(mesh):
    return jax.shard_map(
        body,
        mesh=mesh,
        in_specs=(
            P("rep", "grp", None), P(), P(),
            P(("grp", "rep"), None), P(("grp", "rep"), None),
            P("grp", "rep", None, None, None), P("grp", "rep", None), P("grp", "rep", None),
            P("rep", "grp"), P(), P(), P(),
        ),
        out_specs=P("grp", "rep", None),
        check_vma=False,
    )
```

```python
import jax
import jax.numpy as jnp
from jax import lax
from jax.experimental import pallas as pl
from jax.experimental.pallas import tpu as pltpu
from jax.sharding import PartitionSpec as P

MESH = pl.DeviceIdType.MESH
DMA = pltpu.SemaphoreType.DMA
BF16 = jnp.bfloat16
F32 = jnp.float32

CAP = 16
STEPS = 128
GROUP = 8
EARLY = 3
PARTS = (0, 80, 112, 128)
CHUNKS = len(PARTS) - 1
TABLE_CHUNKS = 8
TILE = 1024


def remote(src, dst, send, recv, device):
    return pltpu.make_async_remote_copy(
        src_ref=src, dst_ref=dst, send_sem=send, recv_sem=recv, device_id=device, device_id_type=MESH
    )


def dot(a, b):
    return jnp.dot(a, b, preferred_element_type=F32)


def item_places(sources, z, y, x, c):
    owner, k = sources // CAP, sources % CAP
    og, o_r = owner // 8, owner % 8
    dz, dy = (z - og // 4 + 4) % 4, (y - og % 4 + 4) % 4
    dx, dc = (x - o_r // 2 + 4) % 4, (c - o_r % 2 + 2) % 2
    a, b, e = dx, (dy - dx + 4) % 4, (dz - dy + 4) % 4
    return ((e * 16 + b * 4 + a) * 2 + dc) * CAP + k


def request_places(requests, z, y):
    og = requests // 256
    slot = ((z - og // 4 + 4) % 4) * 4 + (y - og % 4 + 4) % 4
    return (requests // 128) % 2 * 2048 + slot * 128 + requests % 128


def to_columns(places, columns):
    wide = places.astype(F32)
    for k in range(places.shape[0]):
        row = jnp.broadcast_to(wide[k : k + 1, :], (128, 128))
        columns[128 * k : 128 * (k + 1), :] = row.T


def onehot(column, first, width):
    lanes = lax.broadcasted_iota(jnp.int32, (1, 128), 1).astype(F32)
    parts = [
        jnp.where(column == lanes + (first + 128 * k), 1.0, 0.0).astype(BF16) for k in range(width // 128)
    ]
    return jnp.concatenate(parts, axis=1)


def ranking_kernel(
    feats_ref, tower_in_ref, tower_out_ref, table_a_ref, table_b_ref, asks_ref, src_ref, req_ref,
    cross_w_ref, cross_b_ref, head_ref, logits_ref,
    src, req, cross_b, head_vmem, tables, stage, ids_half, ids_mine, ids_smem, send_rows, recv_rows, rows_wide, feats_all,
    cross_w, tower_in, tower_out, flipped, src_col, req_smem, user, rows_a, items,
    small_sem, table_sem, weight_sem, local_sem, ids_send, ids_recv, ag_send, ag_recv, row_send, row_recv,
):
    g, r = lax.axis_index("grp"), lax.axis_index("rep")
    z, y, x, c = g // 4, g % 4, r // 2, r % 2
    g_line = [(g + i) % 16 for i in range(16)]
    r_line = [(r + i) % 8 for i in range(8)]
    y_line = [z * 4 + (y + i) % 4 for i in range(4)]
    z_line = [((z + i) % 4) * 4 + y for i in range(4)]

    span = tables.shape[0] // TABLE_CHUNKS
    small_copies = [
        pltpu.make_async_copy(ref, scratch, small_sem.at[n])
        for n, (ref, scratch) in enumerate(
            (
                (feats_ref.at[0, pl.ds(0, 128)], feats_all.at[0]),
                (feats_ref.at[0, pl.ds(128, 128)], feats_all.at[16]),
                (src_ref, src),
                (req_ref, req),
                (cross_b_ref, cross_b),
                (head_ref, head_vmem),
            )
        )
    ]
    for copy in small_copies:
        copy.start()

    barrier = pltpu.get_barrier_semaphore()
    for i in range(1, 8):
        pl.semaphore_signal(barrier, inc=1, device_id=(g, r_line[i]), device_id_type=MESH)
    for i in range(1, 16):
        pl.semaphore_signal(barrier, inc=1, device_id=(g_line[i], r), device_id_type=MESH)

    table_copies = []
    for k in range(TABLE_CHUNKS):
        for t, ref in enumerate((table_a_ref, table_b_ref)):
            table_copies.append(
                pltpu.make_async_copy(
                    ref.at[pl.ds(k * span, span)], stage.at[t, pl.ds(k * span, span)], table_sem.at[t, k]
                )
            )
    for copy in table_copies:
        copy.start()
    weight_copies = [
        pltpu.make_async_copy(ref, scratch, weight_sem.at[n])
        for n, (ref, scratch) in enumerate(
            ((tower_in_ref, tower_in), (tower_out_ref, tower_out), (cross_w_ref, cross_w))
        )
    ]
    for copy in weight_copies:
        copy.start()

    for copy in small_copies:
        copy.wait()
    pl.semaphore_wait(barrier, 22)

    first = [remote(asks_ref.at[:, r_line[i]], ids_half.at[:, r], ids_send.at[0], ids_recv.at[0], (g, r_line[i])) for i in range(1, 8)]
    for copy in first:
        copy.start()
    own = pltpu.make_async_copy(asks_ref.at[:, r], ids_half.at[:, r], local_sem.at[0])
    own.start()
    def block(h, first, second):
        return 4 * second + first if h == 0 else 16 + 4 * first + second

    def hand_on(h, at, to, leg, hop, part=None):
        line = (y_line, z_line)[h if leg == 0 else 1 - h]
        rows = pl.ds(0, 128) if part is None else pl.ds(64 * part, 64)
        a, b = block(h, *at), block(h, *to)
        remote(feats_all.at[a, rows], feats_all.at[b, rows], ag_send, ag_recv.at[b], (line[hop], r)).start()

    def have(h, first, second):
        part = feats_all.at[block(h, first, second)]
        pltpu.make_async_copy(part, part, ag_recv.at[block(h, first, second)]).wait()

    def to_both(h, first):
        for hop in (1, 3):
            hand_on(h, (first, 0), (first, hop), 1, hop)

    for h in range(2):
        for hop in (1, 3):
            hand_on(h, (0, 0), (hop, 0), 0, hop)
    for h in range(2):
        to_both(h, 0)

    for k in range(TABLE_CHUNKS):
        for t in range(2):
            table_copies[2 * k + t].wait()

        @pl.loop(0, span // 64)
        def _(j):
            at = pl.multiple_of(k * span + j * 64, 64)
            tables[pl.ds(at, 64), 0:256] = stage[0, pl.ds(at, 64), :].astype(F32)
            tables[pl.ds(at, 64), 256:512] = stage[1, pl.ds(at, 64), :].astype(F32)

    own.wait()
    pltpu.make_async_copy(ids_half.at[:, pl.ds(0, 7)], ids_half.at[:, pl.ds(0, 7)], ids_recv.at[0]).wait()
    for i in range(1, 16):
        remote(ids_half.at[g_line[i]], ids_mine.at[g], ids_send.at[1], ids_recv.at[1], (g_line[i], r)).start()
    own = pltpu.make_async_copy(ids_half.at[g], ids_mine.at[g], local_sem.at[0])
    own.start()
    for n, hop in enumerate((1, 3)):
        for h in range(2):
            have(h, hop, 0)
            hand_on(h, (hop, 0), (2, 0), 0, hop, n)
            to_both(h, hop)
    for n, hop in enumerate((1, 3)):
        for h in range(2):
            have(h, 0, hop)
            hand_on(h, (0, hop), (0, 2), 1, hop, n)

    slots, half = user.shape
    width = half // 2
    bias = cross_b[...]
    head = head_vmem[...].astype(F32).reshape(1, 2 * half)
    req[...] = request_places(req[...], z, y)
    to_smem = pltpu.make_async_copy(req, req_smem, local_sem.at[1])
    to_smem.start()
    to_columns(item_places(src[...], z, y, x, c), src_col)
    to_smem.wait()

    for h in range(2):
        have(h, 2, 0)
        to_both(h, 2)
    for first in (1, 3):
        for n, hop in enumerate((1, 3)):
            for h in range(2):
                have(h, first, hop)
                hand_on(h, (first, hop), (first, 2), 1, hop, n)

    own.wait()
    pltpu.make_async_copy(ids_half.at[pl.ds(0, 15)], ids_mine.at[pl.ds(0, 15)], ids_recv.at[1]).wait()
    to_smem = pltpu.make_async_copy(ids_mine, ids_smem, local_sem.at[1])
    to_smem.start()
    to_smem.wait()

    r_hops = [((x + hop) % 4) * 2 + (c + dc) % 2 for hop in range(4) for dc in range(2)]

    def partner(j, m):
        hop_y = m // 2 + j % 4
        hop_z = hop_y + j // 4
        return ((z + hop_z) % 4) * 4 + (y + hop_y) % 4, r_hops[m]

    def gather(j):
        for m in range(GROUP):
            to_g, to_r = partner(j, m)
            for k in range(CAP):
                rows_wide[m, pl.ds(k, 1), :] = tables[pl.ds(ids_smem[to_g, to_r, 0, k], 1), :]
            send_rows[j * GROUP + m] = rows_wide[m].astype(BF16)

    def send(j, n, sem, first=0):
        for m in range(first, GROUP):
            i = j * GROUP + m
            columns = pl.ds(n * width, width)
            remote(
                send_rows.at[i, :, columns], recv_rows.at[i, :, columns], row_send, row_recv.at[sem], partner(j, m)
            ).start()

    @pl.loop(0, 1)
    def _(j):
        gather(j)

    for n, hop in enumerate((1, 3)):
        for h in range(2):
            have(h, 2, hop)
            hand_on(h, (2, hop), (2, 2), 1, hop, n)

    @pl.loop(1, EARLY)
    def _(j):
        gather(j)

    for first in (0, 1, 3):
        for h in range(2):
            have(h, first, 2)

    recv_rows[0] = send_rows[0]
    send(0, 0, CHUNKS, 1)

    @pl.loop(1, EARLY)
    def _(j):
        send(j, 0, CHUNKS)

    @pl.loop(EARLY, STEPS // GROUP)
    def _(j):
        gather(j)
        send(j, 0, CHUNKS)

    def arrived(first, last, columns, sem):
        part = recv_rows.at[pl.ds(max(first, 1), last - max(first, 1)), :, columns]
        pltpu.make_async_copy(part, part, row_recv.at[sem]).wait()

    def tile(t, first=0):
        return pl.ds(pl.multiple_of(first + t * TILE, TILE), TILE)

    def picked(t, k):
        first, count = PARTS[k] * CAP, (PARTS[k + 1] - PARTS[k]) * CAP
        rows = recv_rows[PARTS[k] : PARTS[k + 1], :, width:].reshape(count, width)
        return dot(onehot(src_col[tile(t), :], first, count), rows)

    def pick_part(k):
        arrived(PARTS[k], PARTS[k + 1], pl.ds(width, width), k)

        @pl.loop(0, slots // TILE)
        def _(t):
            items[tile(t), :] = picked(t, k) if k == 0 else items[tile(t), :] + picked(t, k)

    for copy in weight_copies:
        copy.wait()
    flipped[...] = (cross_w[2].astype(F32) * head).T.astype(BF16)

    for h in range(2):
        have(h, 2, 2)

    e = width

    @pl.loop(0, 32)
    def _(j):
        tables[pl.ds(pl.multiple_of(128 * j, 128), 128), 0:e] = feats_all[j].astype(F32)

    @pl.loop(0, slots // 128)
    def _(j):
        for m in range(8):
            for k in range(16):
                rows_wide[m, pl.ds(k, 1), 0:e] = tables[pl.ds(req_smem[j, 16 * m + k], 1), 0:e]
            user[pl.ds(pl.multiple_of(128 * j, 128) + 16 * m, 16), 0:e] = rows_wide[m, :, 0:e].astype(BF16)

    @pl.loop(0, slots // TILE)
    def _(t):
        hidden = jnp.maximum(dot(user[tile(t), 0:256], tower_in[...]), 0.0).astype(BF16)
        user[tile(t), :] = dot(hidden, tower_out[...]).astype(BF16)

    send(0, 1, 0, 1)
    for k in range(CHUNKS):

        @pl.loop(max(PARTS[k] // GROUP, 1), PARTS[k + 1] // GROUP)
        def _(j):
            send(j, 1, k)

    @pl.loop(0, slots // TILE)
    def _(t):
        for n in range(2):
            cols = slice(half * n, half * (n + 1))
            vec = user[tile(t), :]
            tables[tile(t, n * slots), :] = dot(vec, cross_w[0, 0:half, cols]) + (bias[0:1, cols] + 1.0)
            tables[tile(t, (n + 2) * slots), :] = dot(vec, flipped[0:half, cols]) + head[:, cols]

    arrived(0, STEPS, pl.ds(0, width), CHUNKS)

    @pl.loop(0, slots // TILE)
    def _(t):
        rows = recv_rows[:, :, 0:width].reshape(STEPS * CAP, width)
        rows_a[tile(t), :] = dot(onehot(src_col[tile(t), :], 0, STEPS * CAP), rows).astype(BF16)

    @pl.loop(0, slots // TILE)
    def _(t):
        vec = rows_a[tile(t), :]
        for n in range(2):
            cols = slice(half * n, half * (n + 1))
            tables[tile(t, n * slots), :] += dot(vec, cross_w[0, half : half + width, cols])
            tables[tile(t, (n + 2) * slots), :] += dot(vec, flipped[half : half + width, cols])

    for k in range(CHUNKS - 1):
        pick_part(k)
    arrived(PARTS[-2], STEPS, pl.ds(width, width), CHUNKS - 1)

    by_bias = head * bias[2:3, :]

    @pl.loop(0, slots // TILE)
    def _(t):
        item = (items[tile(t), :] + picked(t, CHUNKS - 1)).astype(BF16)
        base = (user[tile(t), :], jnp.concatenate([rows_a[tile(t), :], item], axis=1))
        crossed = []
        for n in range(2):
            cols = slice(half * n, half * (n + 1))
            mixed = dot(item, cross_w[0, half + width :, cols]) + tables[tile(t, n * slots), :]
            crossed.append((base[n].astype(F32) * mixed).astype(BF16))
        crossed_1 = jnp.concatenate(crossed, axis=1)
        total = jnp.zeros((TILE, 128), F32)
        for n in range(2):
            cols = slice(half * n, half * (n + 1))
            wide = base[n].astype(F32)
            mixed = dot(crossed_1, cross_w[1, :, cols]) + bias[1:2, cols]
            crossed_2 = (wide * mixed + crossed[n].astype(F32)).astype(BF16).astype(F32)
            turned = dot(item, flipped[half + width :, cols]) + tables[tile(t, (n + 2) * slots), :]
            score = crossed_2 * turned + wide * by_bias[:, cols]
            for m in range(half // 128):
                total += score[:, 128 * m : 128 * (m + 1)]
        for m in range(TILE // 128):
            logits_ref[pl.ds(t * (TILE // 128) + m, 1), :] = jnp.sum(
                total[128 * m : 128 * (m + 1), :].T, axis=0, keepdims=True
            )

    pltpu.make_async_copy(ids_half.at[:, pl.ds(0, 7)], ids_half.at[:, pl.ds(0, 7)], ids_send.at[0]).wait()
    pltpu.make_async_copy(ids_half.at[pl.ds(0, 15)], ids_mine.at[pl.ds(0, 15)], ids_send.at[1]).wait()
    pltpu.make_async_copy(feats_all.at[pl.ds(0, 30)], feats_all.at[pl.ds(0, 30)], ag_send).wait()
    part = send_rows.at[pl.ds(0, STEPS - 1)]
    pltpu.make_async_copy(part, part, row_send).wait()


def body(
    user_feats, tower_in, tower_out, table_a, table_b, ask_rows, slot_src, slot_req, live_counts, cross_w, cross_b, head_w,
):
    vmem = pl.BlockSpec(memory_space=pltpu.VMEM)
    anywhere = pl.BlockSpec(memory_space=pl.ANY)
    rows_dev, e = table_a.shape
    slots = slot_src.shape[-1]
    x = cross_w.shape[-1]
    logits = pl.pallas_call(
        ranking_kernel,
        out_shape=jax.ShapeDtypeStruct((slots // 128, 128), F32),
        in_specs=[anywhere] * 11,
        out_specs=vmem,
        scratch_shapes=[
            pltpu.VMEM((slots // 128, 128), jnp.int32),
            pltpu.VMEM((slots // 128, 128), jnp.int32),
            pltpu.VMEM(cross_b.shape, F32),
            pltpu.VMEM(head_w.shape, BF16),
            pltpu.VMEM((rows_dev, 2 * e), F32),
            pltpu.VMEM((2, rows_dev, e), BF16),
            pltpu.VMEM((16, 8, 1, CAP), jnp.int32),
            pltpu.VMEM((16, 8, 1, CAP), jnp.int32),
            pltpu.SMEM((16, 8, 1, CAP), jnp.int32),
            pltpu.VMEM((STEPS, CAP, 2 * e), BF16),
            pltpu.VMEM((STEPS, CAP, 2 * e), BF16),
            pltpu.VMEM((GROUP, CAP, 2 * e), F32),
            pltpu.VMEM((32, 128, user_feats.shape[-1]), BF16),
            pltpu.VMEM(cross_w.shape, BF16),
            pltpu.VMEM(tower_in.shape, BF16),
            pltpu.VMEM(tower_out.shape, BF16),
            pltpu.VMEM((x, x), BF16),
            pltpu.VMEM((slots, 128), F32),
            pltpu.SMEM((slots // 128, 128), jnp.int32),
            pltpu.VMEM((slots, x // 2), BF16),
            pltpu.VMEM((slots, e), BF16),
            pltpu.VMEM((slots, e), F32),
            DMA((6,)),
            DMA((2, TABLE_CHUNKS)),
            DMA((3,)),
            DMA((2,)),
            DMA((2,)),
            DMA((2,)),
            DMA,
            DMA((32,)),
            DMA,
            DMA((CHUNKS + 1,)),
        ],
        compiler_params=pltpu.CompilerParams(
            collective_id=0, has_side_effects=True, vmem_limit_bytes=60 * 1024 * 1024
        ),
    )(
        user_feats, tower_in, tower_out, table_a, table_b, ask_rows.reshape(16, 8, 1, CAP),
        slot_src.reshape(slots // 128, 128), slot_req.reshape(slots // 128, 128),
        cross_w, cross_b, head_w,
    )
    live = lax.broadcasted_iota(jnp.int32, (1, 1, slots), 2) < live_counts[0, 0]
    return jnp.where(live, logits.reshape(1, 1, slots), 0.0)


def solution(mesh):
    return jax.shard_map(
        body,
        mesh=mesh,
        in_specs=(
            P("rep", "grp", None), P(), P(),
            P(("grp", "rep"), None), P(("grp", "rep"), None),
            P("grp", "rep", None, None, None), P("grp", "rep", None), P("grp", "rep", None),
            P("rep", "grp"), P(), P(), P(),
        ),
        out_specs=P("grp", "rep", None),
        check_vma=False,
    )
```

```python
import jax
import jax.numpy as jnp
from jax import lax
from jax.experimental import pallas as pl
from jax.experimental.pallas import tpu as pltpu
from jax.sharding import PartitionSpec as P

MESH = pl.DeviceIdType.MESH
DMA = pltpu.SemaphoreType.DMA
BF16 = jnp.bfloat16
F32 = jnp.float32

CAP = 16
STEPS = 128
GROUP = 8
EARLY = 3
PARTS = (0, 80, 112, 128)
CHUNKS = len(PARTS) - 1
TABLE_CHUNKS = 8
TILE = 1024


def remote(src, dst, send, recv, device):
    return pltpu.make_async_remote_copy(
        src_ref=src, dst_ref=dst, send_sem=send, recv_sem=recv, device_id=device, device_id_type=MESH
    )


def dot(a, b):
    return jnp.dot(a, b, preferred_element_type=F32)


def item_places(sources, z, y, x, c):
    owner, k = sources // CAP, sources % CAP
    og, o_r = owner // 8, owner % 8
    dz, dy = (z - og // 4 + 4) % 4, (y - og % 4 + 4) % 4
    dx, dc = (x - o_r // 2 + 4) % 4, (c - o_r % 2 + 2) % 2
    a, b, e = dx, (dy - dx + 4) % 4, (dz - dy + 4) % 4
    return ((e * 16 + b * 4 + a) * 2 + dc) * CAP + k


def request_places(requests, z, y):
    og = requests // 256
    slot = ((z - og // 4 + 4) % 4) * 4 + (y - og % 4 + 4) % 4
    return (requests // 128) % 2 * 2048 + slot * 128 + requests % 128


def to_columns(places, columns):
    wide = places.astype(F32)
    for k in range(places.shape[0]):
        row = jnp.broadcast_to(wide[k : k + 1, :], (128, 128))
        columns[128 * k : 128 * (k + 1), :] = row.T


def onehot(column, first, width):
    lanes = lax.broadcasted_iota(jnp.int32, (1, 128), 1).astype(F32)
    parts = [
        jnp.where(column == lanes + (first + 128 * k), 1.0, 0.0).astype(BF16) for k in range(width // 128)
    ]
    return jnp.concatenate(parts, axis=1)


def ranking_kernel(
    feats_ref, tower_in_ref, tower_out_ref, table_a_ref, table_b_ref, asks_ref, src_ref, req_ref,
    cross_w_ref, cross_b_ref, head_ref, logits_ref,
    src, req, cross_b, head_vmem, tables, stage, ids_half, ids_mine, ids_smem, send_rows, recv_rows, rows_wide, feats_all,
    cross_w, tower_in, tower_out, flipped, src_col, req_smem, user, rows_a, items,
    small_sem, table_sem, weight_sem, local_sem, ids_send, ids_recv, ag_send, ag_recv, row_send, row_recv,
):
    g, r = lax.axis_index("grp"), lax.axis_index("rep")
    z, y, x, c = g // 4, g % 4, r // 2, r % 2
    g_line = [(g + i) % 16 for i in range(16)]
    r_line = [(r + i) % 8 for i in range(8)]
    y_line = [z * 4 + (y + i) % 4 for i in range(4)]
    z_line = [((z + i) % 4) * 4 + y for i in range(4)]

    span = tables.shape[0] // TABLE_CHUNKS
    small_copies = [
        pltpu.make_async_copy(ref, scratch, small_sem.at[n])
        for n, (ref, scratch) in enumerate(
            (
                (feats_ref.at[0, pl.ds(0, 128)], feats_all.at[0]),
                (feats_ref.at[0, pl.ds(128, 128)], feats_all.at[16]),
                (src_ref, src),
                (req_ref, req),
                (cross_b_ref, cross_b),
                (head_ref, head_vmem),
            )
        )
    ]
    for copy in small_copies:
        copy.start()

    barrier = pltpu.get_barrier_semaphore()
    for i in range(1, 8):
        pl.semaphore_signal(barrier, inc=1, device_id=(g, r_line[i]), device_id_type=MESH)
    for i in range(1, 16):
        pl.semaphore_signal(barrier, inc=1, device_id=(g_line[i], r), device_id_type=MESH)

    table_copies = []
    for k in range(TABLE_CHUNKS):
        for t, ref in enumerate((table_a_ref, table_b_ref)):
            table_copies.append(
                pltpu.make_async_copy(
                    ref.at[pl.ds(k * span, span)], stage.at[t, pl.ds(k * span, span)], table_sem.at[t, k]
                )
            )
    for copy in table_copies:
        copy.start()
    weight_copies = [
        pltpu.make_async_copy(ref, scratch, weight_sem.at[n])
        for n, (ref, scratch) in enumerate(
            ((tower_in_ref, tower_in), (tower_out_ref, tower_out), (cross_w_ref, cross_w))
        )
    ]
    for copy in weight_copies:
        copy.start()

    for copy in small_copies:
        copy.wait()
    pl.semaphore_wait(barrier, 22)

    first = [remote(asks_ref.at[:, r_line[i]], ids_half.at[:, r], ids_send.at[0], ids_recv.at[0], (g, r_line[i])) for i in range(1, 8)]
    for copy in first:
        copy.start()
    own = pltpu.make_async_copy(asks_ref.at[:, r], ids_half.at[:, r], local_sem.at[0])
    own.start()
    def block(h, first, second):
        return 4 * second + first if h == 0 else 16 + 4 * first + second

    def hand_on(h, at, to, leg, hop, part=None):
        line = (y_line, z_line)[h if leg == 0 else 1 - h]
        rows = pl.ds(0, 128) if part is None else pl.ds(64 * part, 64)
        a, b = block(h, *at), block(h, *to)
        remote(feats_all.at[a, rows], feats_all.at[b, rows], ag_send, ag_recv.at[b], (line[hop], r)).start()

    def have(h, first, second):
        part = feats_all.at[block(h, first, second)]
        pltpu.make_async_copy(part, part, ag_recv.at[block(h, first, second)]).wait()

    def to_both(h, first):
        for hop in (1, 3):
            hand_on(h, (first, 0), (first, hop), 1, hop)

    for h in range(2):
        for hop in (1, 3):
            hand_on(h, (0, 0), (hop, 0), 0, hop)
    for h in range(2):
        to_both(h, 0)

    for k in range(TABLE_CHUNKS):
        for t in range(2):
            table_copies[2 * k + t].wait()

        @pl.loop(0, span // 64)
        def _(j):
            at = pl.multiple_of(k * span + j * 64, 64)
            tables[pl.ds(at, 64), 0:256] = stage[0, pl.ds(at, 64), :].astype(F32)
            tables[pl.ds(at, 64), 256:512] = stage[1, pl.ds(at, 64), :].astype(F32)

    own.wait()
    pltpu.make_async_copy(ids_half.at[:, pl.ds(0, 7)], ids_half.at[:, pl.ds(0, 7)], ids_recv.at[0]).wait()
    for i in range(1, 16):
        remote(ids_half.at[g_line[i]], ids_mine.at[g], ids_send.at[1], ids_recv.at[1], (g_line[i], r)).start()
    own = pltpu.make_async_copy(ids_half.at[g], ids_mine.at[g], local_sem.at[0])
    own.start()
    for n, hop in enumerate((1, 3)):
        for h in range(2):
            have(h, hop, 0)
            hand_on(h, (hop, 0), (2, 0), 0, hop, n)
            to_both(h, hop)
    for n, hop in enumerate((1, 3)):
        for h in range(2):
            have(h, 0, hop)
            hand_on(h, (0, hop), (0, 2), 1, hop, n)

    slots, half = user.shape
    width = half // 2
    bias = cross_b[...]
    head = head_vmem[...].astype(F32).reshape(1, 2 * half)
    req[...] = request_places(req[...], z, y)
    to_smem = pltpu.make_async_copy(req, req_smem, local_sem.at[1])
    to_smem.start()
    to_columns(item_places(src[...], z, y, x, c), src_col)
    to_smem.wait()

    for h in range(2):
        have(h, 2, 0)
        to_both(h, 2)
    for first in (1, 3):
        for n, hop in enumerate((1, 3)):
            for h in range(2):
                have(h, first, hop)
                hand_on(h, (first, hop), (first, 2), 1, hop, n)

    own.wait()
    pltpu.make_async_copy(ids_half.at[pl.ds(0, 15)], ids_mine.at[pl.ds(0, 15)], ids_recv.at[1]).wait()
    to_smem = pltpu.make_async_copy(ids_mine, ids_smem, local_sem.at[1])
    to_smem.start()
    to_smem.wait()

    r_hops = [((x + hop) % 4) * 2 + (c + dc) % 2 for hop in range(4) for dc in range(2)]

    def partner(j, m):
        hop_y = m // 2 + j % 4
        hop_z = hop_y + j // 4
        return ((z + hop_z) % 4) * 4 + (y + hop_y) % 4, r_hops[m]

    def gather(j):
        for m in range(GROUP):
            to_g, to_r = partner(j, m)
            for k in range(CAP):
                rows_wide[m, pl.ds(k, 1), :] = tables[pl.ds(ids_smem[to_g, to_r, 0, k], 1), :]
            send_rows[j * GROUP + m] = rows_wide[m].astype(BF16)

    def send(j, n, sem, first=0):
        for m in range(first, GROUP):
            i = j * GROUP + m
            columns = pl.ds(n * width, width)
            remote(
                send_rows.at[i, :, columns], recv_rows.at[i, :, columns], row_send, row_recv.at[sem], partner(j, m)
            ).start()

    @pl.loop(0, 1)
    def _(j):
        gather(j)

    for n, hop in enumerate((1, 3)):
        for h in range(2):
            have(h, 2, hop)
            hand_on(h, (2, hop), (2, 2), 1, hop, n)

    @pl.loop(1, EARLY)
    def _(j):
        gather(j)

    for first in (0, 1, 3):
        for h in range(2):
            have(h, first, 2)

    recv_rows[0] = send_rows[0]
    send(0, 0, CHUNKS, 1)

    @pl.loop(1, EARLY)
    def _(j):
        send(j, 0, CHUNKS)

    @pl.loop(EARLY, STEPS // GROUP)
    def _(j):
        gather(j)
        send(j, 0, CHUNKS)

    def arrived(first, last, columns, sem):
        part = recv_rows.at[pl.ds(max(first, 1), last - max(first, 1)), :, columns]
        pltpu.make_async_copy(part, part, row_recv.at[sem]).wait()

    def tile(t, first=0):
        return pl.ds(pl.multiple_of(first + t * TILE, TILE), TILE)

    def picked(t, k):
        first, count = PARTS[k] * CAP, (PARTS[k + 1] - PARTS[k]) * CAP
        rows = recv_rows[PARTS[k] : PARTS[k + 1], :, width:].reshape(count, width)
        return dot(onehot(src_col[tile(t), :], first, count), rows)

    def pick_part(k):
        arrived(PARTS[k], PARTS[k + 1], pl.ds(width, width), k)

        @pl.loop(0, slots // TILE)
        def _(t):
            items[tile(t), :] = picked(t, k) if k == 0 else items[tile(t), :] + picked(t, k)

    for copy in weight_copies:
        copy.wait()
    flipped[...] = (cross_w[2].astype(F32) * head).T.astype(BF16)

    for h in range(2):
        have(h, 2, 2)

    e = width

    @pl.loop(0, 32)
    def _(j):
        tables[pl.ds(pl.multiple_of(128 * j, 128), 128), 0:e] = feats_all[j].astype(F32)

    @pl.loop(0, slots // 128)
    def _(j):
        for m in range(8):
            for k in range(16):
                rows_wide[m, pl.ds(k, 1), 0:e] = tables[pl.ds(req_smem[j, 16 * m + k], 1), 0:e]
            user[pl.ds(pl.multiple_of(128 * j, 128) + 16 * m, 16), 0:e] = rows_wide[m, :, 0:e].astype(BF16)

    @pl.loop(0, slots // TILE)
    def _(t):
        hidden = jnp.maximum(dot(user[tile(t), 0:256], tower_in[...]), 0.0).astype(BF16)
        user[tile(t), :] = dot(hidden, tower_out[...]).astype(BF16)

    send(0, 1, 0, 1)
    for k in range(CHUNKS):

        @pl.loop(max(PARTS[k] // GROUP, 1), PARTS[k + 1] // GROUP)
        def _(j):
            send(j, 1, k)

    @pl.loop(0, slots // TILE)
    def _(t):
        for n in range(2):
            cols = slice(half * n, half * (n + 1))
            vec = user[tile(t), :]
            tables[tile(t, n * slots), :] = dot(vec, cross_w[0, 0:half, cols]) + (bias[0:1, cols] + 1.0)
            tables[tile(t, (n + 2) * slots), :] = dot(vec, flipped[0:half, cols]) + head[:, cols]

    arrived(0, STEPS, pl.ds(0, width), CHUNKS)

    @pl.loop(0, slots // TILE)
    def _(t):
        rows = recv_rows[:, :, 0:width].reshape(STEPS * CAP, width)
        vec = dot(onehot(src_col[tile(t), :], 0, STEPS * CAP), rows).astype(BF16)
        rows_a[tile(t), :] = vec
        for n in range(2):
            cols = slice(half * n, half * (n + 1))
            tables[tile(t, n * slots), :] += dot(vec, cross_w[0, half : half + width, cols])
            tables[tile(t, (n + 2) * slots), :] += dot(vec, flipped[half : half + width, cols])

    for k in range(CHUNKS - 1):
        pick_part(k)
    arrived(PARTS[-2], STEPS, pl.ds(width, width), CHUNKS - 1)

    by_bias = head * bias[2:3, :]

    @pl.loop(0, slots // TILE, unroll=2)
    def _(t):
        item = (items[tile(t), :] + picked(t, CHUNKS - 1)).astype(BF16)
        base = (user[tile(t), :], jnp.concatenate([rows_a[tile(t), :], item], axis=1))
        crossed = []
        for n in range(2):
            cols = slice(half * n, half * (n + 1))
            mixed = dot(item, cross_w[0, half + width :, cols]) + tables[tile(t, n * slots), :]
            crossed.append((base[n].astype(F32) * mixed).astype(BF16))
        crossed_1 = jnp.concatenate(crossed, axis=1)
        total = jnp.zeros((TILE, 128), F32)
        for n in range(2):
            cols = slice(half * n, half * (n + 1))
            wide = base[n].astype(F32)
            mixed = dot(crossed_1, cross_w[1, :, cols]) + bias[1:2, cols]
            crossed_2 = (wide * mixed + crossed[n].astype(F32)).astype(BF16).astype(F32)
            turned = dot(item, flipped[half + width :, cols]) + tables[tile(t, (n + 2) * slots), :]
            score = crossed_2 * turned + wide * by_bias[:, cols]
            for m in range(half // 128):
                total += score[:, 128 * m : 128 * (m + 1)]
        for m in range(TILE // 128):
            logits_ref[pl.ds(t * (TILE // 128) + m, 1), :] = jnp.sum(
                total[128 * m : 128 * (m + 1), :].T, axis=0, keepdims=True
            )

    pltpu.make_async_copy(ids_half.at[:, pl.ds(0, 7)], ids_half.at[:, pl.ds(0, 7)], ids_send.at[0]).wait()
    pltpu.make_async_copy(ids_half.at[pl.ds(0, 15)], ids_mine.at[pl.ds(0, 15)], ids_send.at[1]).wait()
    pltpu.make_async_copy(feats_all.at[pl.ds(0, 30)], feats_all.at[pl.ds(0, 30)], ag_send).wait()
    part = send_rows.at[pl.ds(0, STEPS - 1)]
    pltpu.make_async_copy(part, part, row_send).wait()


def body(
    user_feats, tower_in, tower_out, table_a, table_b, ask_rows, slot_src, slot_req, live_counts, cross_w, cross_b, head_w,
):
    vmem = pl.BlockSpec(memory_space=pltpu.VMEM)
    anywhere = pl.BlockSpec(memory_space=pl.ANY)
    rows_dev, e = table_a.shape
    slots = slot_src.shape[-1]
    x = cross_w.shape[-1]
    logits = pl.pallas_call(
        ranking_kernel,
        out_shape=jax.ShapeDtypeStruct((slots // 128, 128), F32),
        in_specs=[anywhere] * 11,
        out_specs=vmem,
        scratch_shapes=[
            pltpu.VMEM((slots // 128, 128), jnp.int32),
            pltpu.VMEM((slots // 128, 128), jnp.int32),
            pltpu.VMEM(cross_b.shape, F32),
            pltpu.VMEM(head_w.shape, BF16),
            pltpu.VMEM((rows_dev, 2 * e), F32),
            pltpu.VMEM((2, rows_dev, e), BF16),
            pltpu.VMEM((16, 8, 1, CAP), jnp.int32),
            pltpu.VMEM((16, 8, 1, CAP), jnp.int32),
            pltpu.SMEM((16, 8, 1, CAP), jnp.int32),
            pltpu.VMEM((STEPS, CAP, 2 * e), BF16),
            pltpu.VMEM((STEPS, CAP, 2 * e), BF16),
            pltpu.VMEM((GROUP, CAP, 2 * e), F32),
            pltpu.VMEM((32, 128, user_feats.shape[-1]), BF16),
            pltpu.VMEM(cross_w.shape, BF16),
            pltpu.VMEM(tower_in.shape, BF16),
            pltpu.VMEM(tower_out.shape, BF16),
            pltpu.VMEM((x, x), BF16),
            pltpu.VMEM((slots, 128), F32),
            pltpu.SMEM((slots // 128, 128), jnp.int32),
            pltpu.VMEM((slots, x // 2), BF16),
            pltpu.VMEM((slots, e), BF16),
            pltpu.VMEM((slots, e), F32),
            DMA((6,)),
            DMA((2, TABLE_CHUNKS)),
            DMA((3,)),
            DMA((2,)),
            DMA((2,)),
            DMA((2,)),
            DMA,
            DMA((32,)),
            DMA,
            DMA((CHUNKS + 1,)),
        ],
        compiler_params=pltpu.CompilerParams(
            collective_id=0, has_side_effects=True, vmem_limit_bytes=60 * 1024 * 1024
        ),
    )(
        user_feats, tower_in, tower_out, table_a, table_b, ask_rows.reshape(16, 8, 1, CAP),
        slot_src.reshape(slots // 128, 128), slot_req.reshape(slots // 128, 128),
        cross_w, cross_b, head_w,
    )
    live = lax.broadcasted_iota(jnp.int32, (1, 1, slots), 2) < live_counts[0, 0]
    return jnp.where(live, logits.reshape(1, 1, slots), 0.0)


def solution(mesh):
    return jax.shard_map(
        body,
        mesh=mesh,
        in_specs=(
            P("rep", "grp", None), P(), P(),
            P(("grp", "rep"), None), P(("grp", "rep"), None),
            P("grp", "rep", None, None, None), P("grp", "rep", None), P("grp", "rep", None),
            P("rep", "grp"), P(), P(), P(),
        ),
        out_specs=P("grp", "rep", None),
        check_vma=False,
    )
```
